32 devices in a mesh: grid: 8 (over z, x), cols: 4 (over y, core).
Axes of the slice: x: 2, y: 2, z: 4, core: 2. Of those that a mesh axis runs over, the one named last changes fastest.
Arguments:
- basis: float32 [1024, 3, 16, 1024], P('cols', None, 'grid'), may hold values from -1 to 1
- snapshots: float32 [128, 3, 16, 1024], P('cols', None, 'grid'), may hold values from -60 to 60
- permittivity: float32 [3, 16, 1024], P(None, 'grid'), may hold values from 1 to 10
- labels: int32 [16, 1024], P('grid'), may hold values from 0 to 7
- sigma_table: float32 [8], replicated, may hold values from 0.1 to 10
Outputs:
- new_basis: float32 [128, 3, 16, 1024], P('cols', None, 'grid')
- coefficients: float32 [1024, 128], P('cols')
- cross_terms: float32 [3, 1024, 128], P(None, 'cols')
- block_terms: float32 [3, 128, 128], P(None, 'cols')
The draws below stay inside these ranges and needn't reach their ends.
All inputs are finite; a program needn't handle non-finite values.
Results may differ from the reference program's by a relative error of at most 0.0003.
Values sent between devices are 32-bit elements; how exact they have to be, the bound alone decides.
A program may use at most 128 MiB of HBM per device.

```python
import math
import jax
import jax.numpy as jnp
from jax import lax

NX = 32
NY = 32
K = 1024
M = 128
NREG = 8
NZ = 16
NU = 49152


def basis_values(key):
    basis_key = jax.random.fold_in(key, 5)
    full_shape = (K, 3, NZ, NX * NY)
    values = jnp.clip(jax.random.normal(basis_key, full_shape, jnp.float32), -6.0, 6.0)
    return values * (1.0 / math.sqrt(NU))


def draw_basis(key, part):
    return basis_values(key).astype(jnp.float32)


def draw_snapshots(key, part):
    base_key = jax.random.fold_in(jax.random.fold_in(key, 11), 0)
    scale_key = jax.random.fold_in(jax.random.fold_in(key, 11), 1)
    mix_key = jax.random.fold_in(jax.random.fold_in(key, 11), 3)
    full_shape = (M, 3, NZ, NX * NY)
    basis_now = basis_values(key)
    depth_frac = jnp.arange(NZ, dtype=jnp.float32) / (NZ - 1)
    column_draw = jax.random.uniform(scale_key, (M, 1, 1, 1), jnp.float32)
    noise_level = math.sqrt(K / NU) / 25.0
    mixing = jnp.clip(jax.random.normal(mix_key, (K, M), jnp.float32), -6.0, 6.0)
    values = jnp.clip(jax.random.normal(base_key, full_shape, jnp.float32), -6.0, 6.0)
    depth_scale = 0.2157 * jnp.exp(math.log(10.0) * depth_frac)
    column_scale = 0.3 * jnp.exp(math.log(10.0) * column_draw)
    flat_basis = basis_now.reshape(K, -1)
    in_span = lax.dot_general(mixing, flat_basis, (((0,), (0,)), ((), ())), precision=lax.Precision.HIGHEST, preferred_element_type=jnp.float32)
    in_span = in_span.reshape(full_shape)
    noise_part = noise_level * values * depth_scale[None, None, :, None]
    return ((in_span + noise_part) * column_scale).astype(jnp.float32)


def with_ends(entries, rng, least, top_value):
    index_at = [jax.random.randint(jax.random.fold_in(rng, axis), (), 0, length) for axis, length in enumerate(entries.shape)]
    widest = entries.shape.index(max(entries.shape))
    beside = index_at[:widest] + [(index_at[widest] + 1) % entries.shape[widest]] + index_at[widest + 1:]
    return entries.at[tuple(index_at)].set(least).at[tuple(beside)].set(top_value)


def shard_levels(key, shape, cuts, low, top_value):
    level = 1.0
    for axis_at, parts in cuts:
        heights = jax.random.uniform(jax.random.fold_in(jax.random.fold_in(key, 6), axis_at), (parts,), jnp.float32, low / len(cuts), top_value / len(cuts))
        level = level * jnp.repeat(jnp.exp(heights), shape[axis_at] // parts).reshape((-1,) + (1,) * (len(shape) - 1 - axis_at))
    return level


def setup_inputs(seed: int = 0) -> dict:
    splits = jax.random.split(jax.random.key(seed), 6)
    basis = draw_basis(jax.random.fold_in(splits[5], 71), 0)
    snapshots = draw_snapshots(jax.random.fold_in(splits[5], 71), 0)
    permittivity = jnp.clip(jnp.exp(math.log(10.0) - 2.3025851 * jax.random.uniform(splits[2], (3, NZ, NX * NY), jnp.float32) ** shard_levels(splits[2], (3, NZ, NX * NY), ((1, 8),), -0.2, 0.2)), 1.0, 10.0)
    labels = with_ends(jax.random.randint(splits[3], (NZ, NX * NY), 0, NREG), jax.random.fold_in(splits[3], 1), 0, NREG - 1).astype(jnp.int32)
    sigma_table = jnp.clip(jnp.exp(jax.random.uniform(splits[4], (NREG,), jnp.float32, math.log(0.1), math.log(10.0))), 0.1, 10.0)
    return dict(basis=basis, snapshots=snapshots, permittivity=permittivity, labels=labels, sigma_table=sigma_table)


HIGHEST = lax.Precision.HIGHEST

def cells_dot(left_rows, right_rows):
    left_flat = left_rows.reshape(left_rows.shape[0], -1)
    right_flat = right_rows.reshape(right_rows.shape[0], -1)
    return lax.dot_general(left_flat.astype(jnp.float32), right_flat.astype(jnp.float32), (((1,), (1,)), ((), ())), precision=HIGHEST, preferred_element_type=jnp.float32)

def combine_rows(weights, fields):
    flattened = fields.reshape(fields.shape[0], -1)
    output_rows = lax.dot_general(weights.astype(jnp.float32), flattened.astype(jnp.float32), (((0,), (0,)), ((), ())), precision=HIGHEST, preferred_element_type=jnp.float32)
    return output_rows.reshape((weights.shape[1],) + fields.shape[1:])

def forward_x(field, row_len):
    padding_cols = jnp.zeros(field.shape[:-1] + (row_len,), field.dtype)
    return jnp.concatenate([field[..., row_len:], padding_cols], axis=-1)

def backward_x(field, row_len):
    padding_cols = jnp.zeros(field.shape[:-1] + (row_len,), field.dtype)
    return jnp.concatenate([padding_cols, field[..., :-row_len]], axis=-1)

def forward_y(field, row_len):
    column_pos = lax.broadcasted_iota(jnp.int32, (field.shape[-1],), 0) % row_len
    padding_cols = jnp.zeros(field.shape[:-1] + (1,), field.dtype)
    shifted = jnp.concatenate([field[..., 1:], padding_cols], axis=-1)
    return jnp.where(column_pos != row_len - 1, shifted, 0.0)

def backward_y(field, row_len):
    column_pos = lax.broadcasted_iota(jnp.int32, (field.shape[-1],), 0) % row_len
    padding_cols = jnp.zeros(field.shape[:-1] + (1,), field.dtype)
    shifted = jnp.concatenate([padding_cols, field[..., :-1]], axis=-1)
    return jnp.where(column_pos != 0, shifted, 0.0)

def curl_curl(extended, row_len):
    field_x = extended[:, 0]
    field_y = extended[:, 1]
    field_z = extended[:, 2]

    def middle(field):
        return field[:, 1:-1]

    def plus_x(field):
        return forward_x(field, row_len) - field

    def minus_x(field):
        return field - backward_x(field, row_len)

    def plus_y(field):
        return forward_y(field, row_len) - field

    def minus_y(field):
        return field - backward_y(field, row_len)

    def second_x(field):
        return forward_x(field, row_len) - 2.0 * field + backward_x(field, row_len)

    def second_y(field):
        return forward_y(field, row_len) - 2.0 * field + backward_y(field, row_len)

    def second_z(field):
        return field[:, 2:] - 2.0 * field[:, 1:-1] + field[:, :-2]
    curl_x = -second_y(middle(field_x)) - second_z(field_x) + minus_y(plus_x(middle(field_y))) + plus_x(middle(field_z)) - plus_x(field_z[:, :-2])
    curl_y = -second_x(middle(field_y)) - second_z(field_y) + minus_x(plus_y(middle(field_x))) + plus_y(middle(field_z)) - plus_y(field_z[:, :-2])
    curl_z = -second_x(middle(field_z)) - second_y(middle(field_z)) + minus_x(field_x[:, 2:] - middle(field_x)) + minus_y(field_y[:, 2:] - middle(field_y))
    return jnp.stack([curl_x, curl_y, curl_z], axis=1)

def lookup_sigma(labels, sigma_table):
    region_ids = jnp.arange(sigma_table.shape[0], dtype=jnp.int32)
    picked = jnp.where(labels[None] == region_ids[:, None, None], sigma_table[:, None, None], 0.0)
    return jnp.sum(picked, axis=0)

def reference(basis, snapshots, permittivity, labels, sigma_table):
    unknowns = 3 * NX * NY * NZ
    current = snapshots
    coefficients = jnp.zeros((basis.shape[0], snapshots.shape[0]), jnp.float32)
    for sweep_index in range(2):
        coef_part = cells_dot(basis, current)
        current = current - combine_rows(coef_part, basis)
        coefficients = coefficients + coef_part
    gram_sum = cells_dot(current, current) / unknowns
    lower_factor = jnp.linalg.cholesky(gram_sum)
    identity = jnp.eye(gram_sum.shape[0], dtype=jnp.float32)
    inverse = jax.scipy.linalg.solve_triangular(lower_factor, identity, lower=True)
    new_all = combine_rows(inverse.T, current)
    extended = jnp.pad(new_all, ((0, 0), (0, 0), (1, 1), (0, 0)))
    conductivity = lookup_sigma(labels, sigma_table)
    curl_term = curl_curl(extended, NY)
    mass_term = permittivity[None] * new_all
    loss_term = conductivity[None, None] * new_all
    cross_terms = jnp.stack([cells_dot(basis, curl_term), cells_dot(basis, mass_term), cells_dot(basis, loss_term)], axis=0)
    block_terms = jnp.stack([cells_dot(new_all, curl_term), cells_dot(new_all, mass_term), cells_dot(new_all, loss_term)], axis=0) / unknowns
    return (new_all, coefficients, cross_terms, block_terms)
```

```python
import functools

import jax
import jax.numpy as jnp
from jax import lax
from jax.experimental import pallas as pl
from jax.experimental.pallas import tpu as pltpu
from jax.sharding import PartitionSpec as P

NY = 32
LANES = 128
SUBS = 8
CHUNK = 2
BATCHES = 2
PIVOTS = 4
MESH = pl.DeviceIdType.MESH
F32 = jnp.float32
BF16 = jnp.bfloat16


def split(value):
    high = value.astype(BF16)
    return high, (value - high.astype(F32)).astype(BF16)


def dot_nt(left, right):
    return lax.dot_general(
        left, right, (((1,), (1,)), ((), ())), preferred_element_type=F32
    )


def dot_nn(left, right):
    return lax.dot_general(
        left, right, (((1,), (0,)), ((), ())), preferred_element_type=F32
    )


def exact_dot(dot, left, right):
    rows = left.shape[0]
    stacked = jnp.concatenate(split(left), axis=0)
    high, low = right if isinstance(right, tuple) else split(right)
    total = dot(stacked, high) + dot(stacked, low)
    return total[:rows] + total[rows:]


def inverse_factor(rows):
    count = len(rows)
    size = count * SUBS
    shape = (SUBS, size)
    left = list(rows)
    lane = lax.broadcasted_iota(jnp.int32, shape, 1)
    sub = lax.broadcasted_iota(jnp.int32, shape, 0)
    right = [jnp.where(lane == sub + SUBS * i, 1.0, 0.0).astype(F32) for i in range(count)]

    def spread(value):
        return jnp.broadcast_to(value, shape)

    for k in range(0, size, PIVOTS):
        block, first = divmod(k, SUBS)
        row_l = [spread(left[block][first + t : first + t + 1]) for t in range(PIVOTS)]
        row_r = [spread(right[block][first + t : first + t + 1]) for t in range(PIVOTS)]
        pivot = {
            (s, t): spread(row_l[s][:, k + t : k + t + 1])
            for s in range(PIVOTS)
            for t in range(s + 1)
        }
        scale, factor = [], {}
        for t in range(PIVOTS):
            scale.append(lax.rsqrt(pivot[t, t]))
            row_l[t] = row_l[t] * scale[t]
            row_r[t] = row_r[t] * scale[t]
            for s in range(t + 1, PIVOTS):
                factor[s, t] = pivot[s, t] * scale[t]
            for s in range(t + 1, PIVOTS):
                for u in range(t + 1, s + 1):
                    pivot[s, u] = pivot[s, u] - factor[s, t] * factor[u, t]
                row_l[s] = row_l[s] - factor[s, t] * row_l[t]
                row_r[s] = row_r[s] - factor[s, t] * row_r[t]
        for at in range(block, count):
            inside = at == block
            if not inside or first + PIVOTS < SUBS:
                cols = [spread(left[at][:, k + t : k + t + 1]) for t in range(PIVOTS)]
                for t in range(PIVOTS):
                    cols[t] = cols[t] * scale[t]
                    for s in range(t + 1, PIVOTS):
                        cols[s] = cols[s] - factor[s, t] * cols[t]
                if inside:
                    cols = [jnp.where(sub >= first + PIVOTS, c, 0.0) for c in cols]
                for t in range(PIVOTS):
                    left[at] = left[at] - cols[t] * row_l[t]
                    right[at] = right[at] - cols[t] * row_r[t]
            if inside:
                for t in range(PIVOTS):
                    right[at] = jnp.where(sub == first + t, row_r[t], right[at])
    return right


def remote(src, dst, send_sem, recv_sem, peer):
    return pltpu.make_async_remote_copy(
        src_ref=src,
        dst_ref=dst,
        send_sem=send_sem,
        recv_sem=recv_sem,
        device_id=peer,
        device_id_type=MESH,
    )


class Reduction:
    def __init__(self, refs, n, me, peer):
        self.x, self.slots, self.o, self.sems = refs
        self.n, self.me, self.peer = n, me, peer

    def put(self, at, value):
        blocks = self.x.shape[1]
        self.x[at // blocks, at % blocks] = value

    def get(self, at):
        blocks = self.x.shape[1]
        return self.o[at // blocks, at % blocks]

    def scatter(self):
        def body(k, carry):
            q = lax.rem(self.me + k, self.n)
            remote(
                self.x.at[q], self.slots.at[k - 1], self.sems.at[0], self.sems.at[1], self.peer(q)
            ).start()
            return carry

        lax.fori_loop(1, self.n, body, 0)

    def spread(self):
        whole = remote(self.slots, self.slots, self.sems.at[0], self.sems.at[1], self.peer(self.me))
        whole.wait_recv()
        self.o[self.me] = self.x[self.me] + jnp.sum(self.slots[...], axis=0)

        def body(k, carry):
            q = lax.rem(self.me + k, self.n)
            mine = self.o.at[self.me]
            remote(mine, mine, self.sems.at[2], self.sems.at[3], self.peer(q)).start()
            return carry

        lax.fori_loop(1, self.n, body, 0)
        whole.wait_send()

    def finish(self):
        rest = self.o.at[pl.ds(0, self.n - 1)]
        whole = remote(rest, rest, self.sems.at[2], self.sems.at[3], self.peer(self.me))
        whole.wait_recv()
        whole.wait_send()


def reduction_scratch(n, blocks):
    piece = -(-blocks // n)
    shapes = [(n, piece), (n - 1, piece), (n, piece)]
    return [pltpu.VMEM(s + (SUBS, LANES), F32) for s in shapes] + [pltpu.SemaphoreType.DMA((4,))]


def kernel(dims, b_ref, s_ref, eps_ref, lab_ref, sig_ref, *rest):
    (grid_size, cols, own_b, own_s, tiles) = dims
    chips = cols // 2
    n16 = 2 * grid_size
    width = own_s // BATCHES
    q_rows = width * cols
    total_s = own_s * cols
    chip_b = 2 * own_b
    chunks = tiles // CHUNK
    per_col = 6 * tiles
    unknowns = 3 * tiles * LANES * n16

    (nb_ref, coef_ref, cross_ref, block_ref) = rest[:4]
    refs = list(rest[4:])

    def take(count):
        out = refs[:count]
        del refs[:count]
        return out

    (sland, bland, ssend, bsend, brecv, bhi, blo, p, below, above) = take(10)
    (uown, urecv, acc, ct, t_acc, t_send, t_recv, op_hi, op_lo, p2_hi, p2_lo, coef_t) = take(12)
    (m_acc, inv_ref, nb_own, nb_send, nb_recv, sig) = take(6)
    (loc, s_s, s_r, bm_s, bm_r, u_s, u_r, h_s, h_r, t_s, t_r, n_s, n_r) = take(13)

    g = lax.axis_index("grid")
    d = lax.axis_index("cols")
    chip, core = d // 2, lax.rem(d, 2)
    me = 2 * g + core
    mate = (g, 2 * chip + 1 - core)
    far = [lax.rem(chip + k, chips) for k in range(1, chips)]
    same = [(g, 2 * y + core) for y in far]
    cross = [(g, 2 * y + 1 - core) for y in far]

    def line(q):
        return (q // 2, 2 * chip + lax.rem(q, 2))

    def slab(q):
        return (q, d)

    c_sums = [Reduction(take(4), n16, me, line) for _ in range(2 * BATCHES)]
    t_sums = [Reduction(take(4), grid_size, g, slab) for _ in range(BATCHES)]
    g_sum = Reduction(take(4), n16, me, line)
    m_sum = Reduction(take(4), n16, me, line)

    barrier = pltpu.get_barrier_semaphore()

    def greet(k, carry):
        pl.semaphore_signal(
            barrier, inc=1, device_id=line(lax.rem(me + k, n16)), device_id_type=MESH
        )
        return carry

    lax.fori_loop(1, n16, greet, 0)
    for peer in same + cross:
        pl.semaphore_signal(barrier, inc=1, device_id=peer, device_id_type=MESH)

    s_load = pltpu.make_async_copy(s_ref, sland, loc.at[0])
    b_load = pltpu.make_async_copy(b_ref, bland, loc.at[1])
    s_load.start()
    b_load.start()

    zero = jnp.zeros((3, q_rows, LANES), F32)
    for b in range(BATCHES):
        for edge in (0, tiles + 1):
            for buffer in (p, below, above):
                buffer[b, edge] = zero
    for buffer, end in ((below, 0), (above, n16 - 1)):

        @pl.when(me == end)
        def _():
            for b in range(BATCHES):
                buffer[b] = jnp.zeros(buffer.shape[1:], F32)

    layer_rows = pl.ds(0, 2 * tiles)
    region = lab_ref[layer_rows]
    picked = jnp.zeros(region.shape, F32)
    for k in range(sig_ref.shape[0]):
        picked = jnp.where(region == k, sig_ref[k], picked)
    sig[...] = picked

    pl.semaphore_wait(barrier, n16 - 1 + 2 * (chips - 1))

    def mine_of(first, second):
        return jnp.where(core == 0, first, second), jnp.where(core == 0, second, first)

    s_load.wait()
    s_copies = []
    my_cols = pl.ds(pl.multiple_of(d * width, SUBS), width)
    for b in range(BATCHES):

        def sort_s(t, carry):
            for a in range(3):
                layers = []
                for layer in range(2):
                    start = b * width * per_col + (2 * tiles * a + layer) + 2 * t
                    layers.append(sland[pl.ds(start, width, stride=per_col), :])
                own, other = mine_of(*layers)
                p[b, t + 1, a, my_cols, :] = own
                ssend[b, t, a] = other
            return carry

        lax.fori_loop(0, tiles, sort_s, 0)
        landing = p.at[b, pl.ds(1, tiles), :, my_cols, :]
        plan = [(landing, peer) for peer in same]
        plan += [(ssend.at[b], peer) for peer in cross + [mate]]
        for i, (src, peer) in enumerate(plan):
            copy = remote(src, landing, s_s.at[b, i], s_r.at[b, i], peer)
            copy.start()
            s_copies.append((b, copy))

    b_load.wait()

    def b_rows(which):
        return pl.ds(pl.multiple_of(which * own_b, own_b), own_b)

    def put_b(t, a, which, value):
        high, low = split(value)
        lanes = pl.ds(pl.multiple_of((lax.rem(t, CHUNK) * 3 + a) * LANES, LANES), LANES)
        bhi[t // CHUNK, b_rows(which), lanes] = high
        blo[t // CHUNK, b_rows(which), lanes] = low

    def sort_b(t, carry):
        for a in range(3):
            layers = []
            for layer in range(2):
                start = (2 * tiles * a + layer) + 2 * t
                layers.append(bland[pl.ds(start, own_b, stride=per_col), :])
            own, other = mine_of(*layers)
            bsend[t, a] = other
            put_b(t, a, core, own)
        remote(bsend.at[t], brecv.at[t], bm_s.at[t], bm_r.at[t], mate).start()
        return carry

    lax.fori_loop(0, tiles, sort_b, 0)

    def mate_b(t, carry):
        remote(bsend.at[t], brecv.at[t], bm_s.at[t], bm_r.at[t], mate).wait()
        for a in range(3):
            put_b(t, a, 1 - core, brecv[t, a])
        return carry

    lax.fori_loop(0, tiles, mate_b, 0)

    def field_chunk(buffer, j):
        parts = [
            buffer[CHUNK * j + i // 3 + 1, i % 3] for i in range(3 * CHUNK)
        ]
        return jnp.concatenate(parts, axis=1)

    def put_coef(total, sweep, b):
        work = c_sums[sweep * BATCHES + b]
        per_row = chip_b // LANES
        for i in range(q_rows // SUBS):
            for k in range(per_row):
                work.put(
                    i * per_row + k,
                    total[SUBS * i : SUBS * (i + 1), LANES * k : LANES * (k + 1)],
                )
        work.scatter()

    def get_coef(sweep, b):
        work = c_sums[sweep * BATCHES + b]
        work.finish()
        per_row = chip_b // LANES
        rows = []
        for i in range(q_rows // SUBS):
            rows.append(
                jnp.concatenate([work.get(i * per_row + k) for k in range(per_row)], axis=1)
            )
        ct[sweep, b] = jnp.concatenate(rows, axis=0)

    def first_coef(b):
        acc[...] = jnp.zeros_like(acc)

        def body(j, carry):
            acc[...] += exact_dot(dot_nt, field_chunk(p.at[b], j), (bhi[j], blo[j]))
            return carry

        lax.fori_loop(0, chunks, body, 0)
        put_coef(acc[...], 0, b)

    def u_copy(sweep, b, j, k):
        part = pl.ds(CHUNK * j, CHUNK)
        return remote(
            uown.at[sweep, b, part],
            urecv.at[sweep, b, k, part],
            u_s.at[sweep, b, k, j],
            u_r.at[sweep, b, k, j],
            same[k],
        )

    def combine(sweep, b):
        weights = ct[sweep, b]

        def body(j, carry):
            u = exact_dot(dot_nn, weights, (bhi[j], blo[j]))
            for i in range(3 * CHUNK):
                uown[sweep, b, CHUNK * j + i // 3, i % 3] = u[:, LANES * i : LANES * (i + 1)]
            for k in range(chips - 1):
                u_copy(sweep, b, j, k).start()
            return carry

        lax.fori_loop(0, chunks, body, 0)

    def remove(sweep, b, j):
        for k in range(chips - 1):
            u_copy(sweep, b, j, k).wait()
        parts = []
        for i in range(3 * CHUNK):
            t, a = CHUNK * j + i // 3, i % 3
            total = uown[sweep, b, t, a]
            for k in range(chips - 1):
                total = total + urecv[sweep, b, k, t, a]
            left = p[b, t + 1, a] - total
            p[b, t + 1, a] = left
            parts.append(left)
        return parts

    def second_coef(b):
        acc[...] = jnp.zeros_like(acc)

        def body(j, carry):
            field = jnp.concatenate(remove(0, b, j), axis=1)
            acc[...] += exact_dot(dot_nt, field, (bhi[j], blo[j]))
            return carry

        lax.fori_loop(0, chunks, body, 0)
        put_coef(acc[...], 1, b)

    def halo(b, j, up):
        part = pl.ds(CHUNK * j + 1, CHUNK)
        comps = pl.ds(0, 3 if up else 2)
        return remote(
            p.at[b, part, comps],
            (below if up else above).at[b, part, comps],
            h_s.at[b, 0 if up else 1, j],
            h_r.at[b, 0 if up else 1, j],
            line(me + 1 if up else me - 1),
        )

    def final_fields(b):
        def body(j, carry):
            remove(1, b, j)

            @pl.when(me < n16 - 1)
            def _():
                halo(b, j, True).start()

            @pl.when(me > 0)
            def _():
                halo(b, j, False).start()

            return carry

        lax.fori_loop(0, chunks, body, 0)

    def halo_wait(b):
        def body(j, carry):
            @pl.when(me > 0)
            def _():
                halo(b, j, True).wait_recv()
                halo(b, j, False).wait_send()

            @pl.when(me < n16 - 1)
            def _():
                halo(b, j, False).wait_recv()
                halo(b, j, True).wait_send()

            return carry

        lax.fori_loop(0, chunks, body, 0)

    lane = lax.broadcasted_iota(jnp.int32, (q_rows, LANES), 1)
    y_at = lax.rem(lane, NY)

    def yp(f):
        return jnp.where(y_at != NY - 1, pltpu.roll(f, LANES - 1, 1), 0.0)

    def ym(f):
        return jnp.where(y_at != 0, pltpu.roll(f, 1, 1), 0.0)

    def xp(f, after):
        return pltpu.roll(jnp.where(lane < NY, after, f), LANES - NY, 1)

    def xm(f, before):
        return pltpu.roll(jnp.where(lane >= LANES - NY, before, f), NY, 1)

    def curl_tile(b, t):
        at = t + 1
        ex, ey, ez = (p[b, at, a] for a in range(3))
        ex_b, ey_b, ez_b = (p[b, at - 1, a] for a in range(3))
        ey_n, ez_n = p[b, at + 1, 1], p[b, at + 1, 2]
        dx, dy, dz = (below[b, at, a] for a in range(3))
        ux, uy = above[b, at, 0], above[b, at, 1]
        w = ez - dz
        w_n = ez_n - below[b, at + 1, 2]
        ey_x = xp(ey, ey_n)
        v = ey_x - ey
        image_x = 4.0 * ex - yp(ex) - ym(ex + v) + v - ux - dx + xp(w, w_n) - w
        h = ex - xm(ex, ex_b) + w
        image_y = 4.0 * ey - ey_x - xm(ey, ey_b) - uy - dy + yp(h) - h
        du = ux - ex
        du_b = above[b, at - 1, 0] - ex_b
        dv = uy - ey
        image_z = (
            4.0 * ez
            - xp(ez, ez_n)
            - yp(ez)
            - xm(ez + du, ez_b + du_b)
            - ym(ez + dv)
            + du
            + dv
        )
        return [image_x, image_y, image_z]

    def layer_row(ref, row):
        return jnp.where(core == 0, ref[pl.ds(row, 1), :], ref[pl.ds(row + 1, 1), :])

    def operators(b):
        t_acc[...] = jnp.zeros_like(t_acc)

        def body(j, carry):
            images = [[], [], []]
            for c in range(CHUNK):
                t = CHUNK * j + c
                images[0] += curl_tile(b, t)
                loss = layer_row(sig, 2 * t)
                for a in range(3):
                    field = p[b, t + 1, a]
                    images[1].append(field * layer_row(eps_ref, 2 * tiles * a + 2 * t))
                    images[2].append(field * loss)
            stack = jnp.concatenate([jnp.concatenate(i, axis=1) for i in images], axis=0)
            high, low = split(stack)
            op_hi[b, j] = high
            op_lo[b, j] = low
            t_acc[...] += dot_nt(high, bhi[j]) + dot_nt(high, blo[j]) + dot_nt(low, bhi[j])
            return carry

        lax.fori_loop(0, chunks, body, 0)

    def t_copy(b):
        return remote(t_send.at[b], t_recv.at[b], t_s.at[b], t_r.at[b], mate)

    def t_start(b):
        for k in range(3):
            total = t_acc[q_rows * k : q_rows * (k + 1)]
            t_send[b, k] = jnp.where(core == 0, total[:, own_b:], total[:, :own_b])
        t_copy(b).start()

    per_own = own_b // LANES

    def t_scatter(b):
        t_copy(b).wait()
        for k in range(3):
            total = t_acc[q_rows * k : q_rows * (k + 1)]
            mine = jnp.where(core == 0, total[:, :own_b], total[:, own_b:]) + t_recv[b, k]
            for i in range(q_rows // SUBS):
                for c in range(per_own):
                    t_sums[b].put(
                        (k * (q_rows // SUBS) + i) * per_own + c,
                        mine[SUBS * i : SUBS * (i + 1), LANES * c : LANES * (c + 1)],
                    )
        t_sums[b].scatter()

    def in_order(parts):
        rows = []
        for e in range(cols):
            for part in parts:
                rows.append(part[width * e : width * (e + 1)])
        return jnp.concatenate(rows, axis=0)

    def s_wait(b):
        for at, copy in s_copies:
            if at == b:
                copy.wait()

    s_wait(0)
    first_coef(0)
    c_sums[0].spread()
    get_coef(0, 0)
    combine(0, 0)
    s_wait(1)
    first_coef(1)
    c_sums[1].spread()
    get_coef(0, 1)
    combine(0, 1)
    second_coef(0)
    c_sums[2].spread()
    get_coef(1, 0)
    combine(1, 0)
    second_coef(1)
    c_sums[3].spread()
    get_coef(1, 1)
    combine(1, 1)

    coef_t[...] = in_order([ct[0, b] + ct[1, b] for b in range(BATCHES)])
    picked = jnp.where(core == 0, coef_t[:, :own_b], coef_t[:, own_b:])
    coef_ref[...] = picked.T

    final_fields(0)
    halo_wait(0)
    operators(0)
    t_start(0)
    t_scatter(0)
    t_sums[0].spread()

    final_fields(1)

    def gram_body(j, carry):
        field = in_order([field_chunk(p.at[b], j) for b in range(BATCHES)])
        high, low = split(field)
        p2_hi[j] = high
        p2_lo[j] = low
        return carry + dot_nt(high, high) + dot_nt(high, low) + dot_nt(low, high)

    gram = lax.fori_loop(0, chunks, gram_body, jnp.zeros((total_s, total_s), F32))
    for i in range(total_s // SUBS):
        g_sum.put(i, gram[SUBS * i : SUBS * (i + 1)])
    g_sum.scatter()
    halo_wait(1)
    operators(1)
    g_sum.spread()
    t_start(1)

    def m_body(j, carry):
        high, low = p2_hi[j], p2_lo[j]
        for b in range(BATCHES):
            m_acc[b] += (
                dot_nt(op_hi[b, j], high) + dot_nt(op_hi[b, j], low) + dot_nt(op_lo[b, j], high)
            )
        return carry

    m_acc[...] = jnp.zeros_like(m_acc)
    lax.fori_loop(0, chunks, m_body, 0)
    for k in range(3):
        rows = in_order([m_acc[b, q_rows * k : q_rows * (k + 1)] for b in range(BATCHES)])
        for i in range(total_s // SUBS):
            m_sum.put(k * (total_s // SUBS) + i, rows[SUBS * i : SUBS * (i + 1)])
    t_scatter(1)
    m_sum.scatter()
    g_sum.finish()
    gram_rows = [g_sum.get(i) * (1.0 / unknowns) for i in range(total_s // SUBS)]
    for i, value in enumerate(inverse_factor(gram_rows)):
        inv_ref[SUBS * i : SUBS * (i + 1)] = value
    t_sums[1].spread()
    m_sum.spread()

    def own_rows(which):
        return pl.ds(pl.multiple_of(which * own_s, SUBS), own_s)

    inv_own = inv_ref[own_rows(d), :]
    inv_mate = inv_ref[own_rows(2 * chip + 1 - core), :]
    inv_chip = jnp.concatenate([inv_own, inv_mate], axis=0)

    def nb_copy(j):
        part = pl.ds(CHUNK * j, CHUNK)
        return remote(nb_send.at[part], nb_recv.at[part], n_s.at[j], n_r.at[j], mate)

    def nb_body(j, carry):
        value = exact_dot(dot_nn, inv_chip, (p2_hi[j], p2_lo[j]))
        for i in range(3 * CHUNK):
            t, a = CHUNK * j + i // 3, i % 3
            part = value[:, LANES * i : LANES * (i + 1)]
            nb_own[t, a] = part[:own_s]
            nb_send[t, a] = part[own_s:]
        nb_copy(j).start()
        return carry

    lax.fori_loop(0, chunks, nb_body, 0)
    inverse = inv_ref[...]
    inverse_halves = split(inverse)
    for b in range(BATCHES):
        t_sums[b].finish()
    for k in range(3):
        parts = []
        for b in range(BATCHES):
            rows = []
            for i in range(q_rows // SUBS):
                at = (k * (q_rows // SUBS) + i) * per_own
                rows.append(
                    jnp.concatenate([t_sums[b].get(at + c) for c in range(per_own)], axis=1)
                )
            parts.append(jnp.concatenate(rows, axis=0))
        cross_ref[k] = exact_dot(dot_nn, inverse, in_order(parts)).T
    m_sum.finish()
    for k in range(3):
        rows = [m_sum.get(k * (total_s // SUBS) + i) for i in range(total_s // SUBS)]
        half = exact_dot(dot_nn, inv_own, jnp.concatenate(rows, axis=0))
        block_ref[k] = exact_dot(dot_nt, half, inverse_halves) * (1.0 / unknowns)

    def nb_out(j, carry):
        nb_copy(j).wait()
        for i in range(3 * CHUNK):
            t, a = CHUNK * j + i // 3, i % 3
            layers = mine_of(nb_own[t, a], nb_recv[t, a])
            for layer in range(2):
                start = (2 * tiles * a + layer) + 2 * t
                nb_ref[pl.ds(start, own_s, stride=per_col), :] = layers[layer]
        return carry

    lax.fori_loop(0, chunks, nb_out, 0)


def shards(basis, snapshots, permittivity, labels, sigma_table):
    own_b, own_s = basis.shape[0], snapshots.shape[0]
    layers, layer = basis.shape[2:]
    assert layers == 2
    grid_size, cols = lax.axis_size("grid"), lax.axis_size("cols")
    tiles = layer // LANES
    chips = cols // 2
    n16 = 2 * grid_size
    width = own_s // BATCHES
    q_rows = width * cols
    total_s = own_s * cols
    chip_b = 2 * own_b
    chunks = tiles // CHUNK
    depth = CHUNK * 3 * LANES
    per_col = 6 * tiles

    def rows_of(value):
        lead = value.shape[:-2]
        value = value.reshape(lead + (layers, tiles, LANES))
        return jnp.swapaxes(value, -3, -2).reshape(-1, LANES)

    padded = (BATCHES, tiles + 2, 3, q_rows, LANES)
    scratch = [
        pltpu.VMEM((own_s * per_col, LANES), F32),
        pltpu.VMEM((own_b * per_col, LANES), F32),
        pltpu.VMEM((BATCHES, tiles, 3, width, LANES), F32),
        pltpu.VMEM((tiles, 3, own_b, LANES), F32),
        pltpu.VMEM((tiles, 3, own_b, LANES), F32),
        pltpu.VMEM((chunks, chip_b, depth), BF16),
        pltpu.VMEM((chunks, chip_b, depth), BF16),
        pltpu.VMEM(padded, F32),
        pltpu.VMEM(padded, F32),
        pltpu.VMEM(padded, F32),
        pltpu.VMEM((2, BATCHES, tiles, 3, q_rows, LANES), F32),
        pltpu.VMEM((2, BATCHES, chips - 1, tiles, 3, q_rows, LANES), F32),
        pltpu.VMEM((q_rows, chip_b), F32),
        pltpu.VMEM((2, BATCHES, q_rows, chip_b), F32),
        pltpu.VMEM((3 * q_rows, chip_b), F32),
        pltpu.VMEM((BATCHES, 3, q_rows, own_b), F32),
        pltpu.VMEM((BATCHES, 3, q_rows, own_b), F32),
        pltpu.VMEM((BATCHES, chunks, 3 * q_rows, depth), BF16),
        pltpu.VMEM((BATCHES, chunks, 3 * q_rows, depth), BF16),
        pltpu.VMEM((chunks, total_s, depth), BF16),
        pltpu.VMEM((chunks, total_s, depth), BF16),
        pltpu.VMEM((total_s, chip_b), F32),
        pltpu.VMEM((BATCHES, 3 * q_rows, total_s), F32),
        pltpu.VMEM((total_s, total_s), F32),
        pltpu.VMEM((tiles, 3, own_s, LANES), F32),
        pltpu.VMEM((tiles, 3, own_s, LANES), F32),
        pltpu.VMEM((tiles, 3, own_s, LANES), F32),
        pltpu.VMEM((2 * tiles, LANES), F32),
    ]
    sem = pltpu.SemaphoreType.DMA
    scratch += [sem((2,))]
    scratch += [sem((BATCHES, 2 * chips - 1))] * 2
    scratch += [sem((tiles,))] * 2
    scratch += [sem((2, BATCHES, chips - 1, chunks))] * 2
    scratch += [sem((BATCHES, 2, chunks))] * 2
    scratch += [sem((BATCHES,))] * 2
    scratch += [sem((chunks,))] * 2
    vreg = SUBS * LANES
    for _ in range(2 * BATCHES):
        scratch += reduction_scratch(n16, q_rows * chip_b // vreg)
    for _ in range(BATCHES):
        scratch += reduction_scratch(grid_size, 3 * q_rows * own_b // vreg)
    scratch += reduction_scratch(n16, total_s * total_s // vreg)
    scratch += reduction_scratch(n16, 3 * total_s * total_s // vreg)

    vmem = pl.BlockSpec(memory_space=pltpu.VMEM)
    dims = (grid_size, cols, own_b, own_s, tiles)
    new_rows, coefficients, cross_terms, block_terms = pl.pallas_call(
        functools.partial(kernel, dims),
        out_shape=[
            jax.ShapeDtypeStruct((own_s * per_col, LANES), F32),
            jax.ShapeDtypeStruct((own_b, total_s), F32),
            jax.ShapeDtypeStruct((3, own_b, total_s), F32),
            jax.ShapeDtypeStruct((3, own_s, total_s), F32),
        ],
        in_specs=[
            pl.BlockSpec(memory_space=pl.ANY),
            pl.BlockSpec(memory_space=pl.ANY),
            vmem,
            vmem,
            pl.BlockSpec(memory_space=pltpu.SMEM),
        ],
        out_specs=[vmem] * 4,
        scratch_shapes=scratch,
        compiler_params=pltpu.CompilerParams(
            collective_id=0, has_side_effects=True, vmem_limit_bytes=62 << 20
        ),
    )(
        rows_of(basis),
        rows_of(snapshots),
        rows_of(permittivity),
        rows_of(labels),
        sigma_table,
    )
    new_basis = jnp.swapaxes(
        new_rows.reshape(own_s, 3, tiles, layers, LANES), 2, 3
    ).reshape(snapshots.shape)
    return (new_basis, coefficients, cross_terms, block_terms)


def solution(mesh):
    placed = (
        P("cols", None, "grid", None),
        P("cols", None, "grid", None),
        P(None, "grid", None),
        P("grid", None),
        P(),
    )
    return jax.shard_map(
        shards,
        mesh=mesh,
        in_specs=placed,
        out_specs=(
            P("cols", None, "grid", None),
            P("cols", None),
            P(None, "cols", None),
            P(None, "cols", None),
        ),
        check_vma=False,
    )
```

```python
import functools

import jax
import jax.numpy as jnp
from jax import lax
from jax.experimental import pallas as pl
from jax.experimental.pallas import tpu as pltpu
from jax.sharding import PartitionSpec as P

NY = 32
LANES = 128
SUBS = 8
CHUNK = 2
PIVOTS = 4
MESH = pl.DeviceIdType.MESH
F32 = jnp.float32
BF16 = jnp.bfloat16


def split(value):
    high = value.astype(BF16)
    return high, (value - high.astype(F32)).astype(BF16)


def dot_nt(left, right):
    return lax.dot_general(
        left, right, (((1,), (1,)), ((), ())), preferred_element_type=F32
    )


def dot_nn(left, right):
    return lax.dot_general(
        left, right, (((1,), (0,)), ((), ())), preferred_element_type=F32
    )


def exact_dot(dot, left, right):
    rows = left.shape[0]
    stacked = jnp.concatenate(split(left), axis=0)
    high, low = right if isinstance(right, tuple) else split(right)
    total = dot(stacked, high) + dot(stacked, low)
    return total[:rows] + total[rows:]


def inverse_factor(rows, between):
    count = len(rows)
    size = count * SUBS
    shape = (SUBS, size)
    left = list(rows)
    lane = lax.broadcasted_iota(jnp.int32, shape, 1)
    sub = lax.broadcasted_iota(jnp.int32, shape, 0)
    right = [jnp.where(lane == sub + SUBS * i, 1.0, 0.0).astype(F32) for i in range(count)]

    def spread(value):
        return jnp.broadcast_to(value, shape)

    for k in range(0, size, PIVOTS):
        if k == size // 4:
            between()
        block, first = divmod(k, SUBS)
        row_l = [spread(left[block][first + t : first + t + 1]) for t in range(PIVOTS)]
        row_r = [spread(right[block][first + t : first + t + 1]) for t in range(PIVOTS)]
        pivot = {
            (s, t): spread(row_l[s][:, k + t : k + t + 1])
            for s in range(PIVOTS)
            for t in range(s + 1)
        }
        scale, factor = [], {}
        for t in range(PIVOTS):
            scale.append(lax.rsqrt(pivot[t, t]))
            row_l[t] = row_l[t] * scale[t]
            row_r[t] = row_r[t] * scale[t]
            for s in range(t + 1, PIVOTS):
                factor[s, t] = pivot[s, t] * scale[t]
            for s in range(t + 1, PIVOTS):
                for u in range(t + 1, s + 1):
                    pivot[s, u] = pivot[s, u] - factor[s, t] * factor[u, t]
                row_l[s] = row_l[s] - factor[s, t] * row_l[t]
                row_r[s] = row_r[s] - factor[s, t] * row_r[t]
        for at in range(block, count):
            inside = at == block
            if not inside or first + PIVOTS < SUBS:
                cols = [spread(left[at][:, k + t : k + t + 1]) for t in range(PIVOTS)]
                for t in range(PIVOTS):
                    cols[t] = cols[t] * scale[t]
                    for s in range(t + 1, PIVOTS):
                        cols[s] = cols[s] - factor[s, t] * cols[t]
                if inside:
                    cols = [jnp.where(sub >= first + PIVOTS, c, 0.0) for c in cols]
                for t in range(PIVOTS):
                    left[at] = left[at] - cols[t] * row_l[t]
                    right[at] = right[at] - cols[t] * row_r[t]
            if inside:
                for t in range(PIVOTS):
                    right[at] = jnp.where(sub == first + t, row_r[t], right[at])
    return right


def remote(src, dst, send_sem, recv_sem, peer):
    return pltpu.make_async_remote_copy(
        src_ref=src,
        dst_ref=dst,
        send_sem=send_sem,
        recv_sem=recv_sem,
        device_id=peer,
        device_id_type=MESH,
    )


class Reduction:
    def __init__(self, refs, n, me, peer):
        self.x, self.slots, self.o, self.sems = refs
        self.n, self.me, self.peer = n, me, peer

    def put(self, at, value):
        blocks = self.x.shape[1]
        self.x[at // blocks, at % blocks] = value

    def get(self, at):
        blocks = self.x.shape[1]
        return self.o[at // blocks, at % blocks]

    def scatter(self):
        def body(k, carry):
            q = lax.rem(self.me + k, self.n)
            remote(
                self.x.at[q], self.slots.at[k - 1], self.sems.at[0], self.sems.at[1], self.peer(q)
            ).start()
            return carry

        lax.fori_loop(1, self.n, body, 0)

    def spread(self):
        whole = remote(self.slots, self.slots, self.sems.at[0], self.sems.at[1], self.peer(self.me))
        whole.wait_recv()
        self.o[self.me] = self.x[self.me] + jnp.sum(self.slots[...], axis=0)

        def body(k, carry):
            q = lax.rem(self.me + k, self.n)
            mine = self.o.at[self.me]
            remote(mine, mine, self.sems.at[2], self.sems.at[3], self.peer(q)).start()
            return carry

        lax.fori_loop(1, self.n, body, 0)
        whole.wait_send()

    def finish(self):
        rest = self.o.at[pl.ds(0, self.n - 1)]
        whole = remote(rest, rest, self.sems.at[2], self.sems.at[3], self.peer(self.me))
        whole.wait_recv()
        whole.wait_send()


def reduction_scratch(n, blocks):
    piece = -(-blocks // n)
    shapes = [(n, piece), (n - 1, piece), (n, piece)]
    return [pltpu.VMEM(s + (SUBS, LANES), F32) for s in shapes] + [pltpu.SemaphoreType.DMA((4,))]


def batch_widths(own_s):
    if own_s % (4 * SUBS) == 0:
        return (own_s // 4, own_s // 2, own_s // 4)
    return (own_s // 2, own_s // 2)


def log2(n):
    bits = n.bit_length() - 1
    assert n == 1 << bits
    return bits


def kernel(dims, b_ref, s_ref, eps_ref, lab_ref, sig_ref, *rest):
    (grid_size, cols, own_b, own_s, tiles) = dims
    chips = cols // 2
    n16 = 2 * grid_size
    bits = log2(n16)
    widths = batch_widths(own_s)
    starts = [sum(widths[:b]) for b in range(len(widths))]
    batches = range(len(widths))
    last = len(widths) - 1
    q_rows = [width * cols for width in widths]
    total_s = own_s * cols
    chip_b = 2 * own_b
    chunks = tiles // CHUNK
    per_col = 6 * tiles
    unknowns = 3 * tiles * LANES * n16

    outs = rest[:4]
    refs = list(rest[4:])

    def take(count):
        out = refs[:count]
        del refs[:count]
        return out

    def each():
        return take(len(widths))

    sland, bland, bsend, brecv, bhi, blo, p2_hi, p2_lo, coef_t, inv_ref = take(10)
    nb_own, nb_send, nb_recv, sig, eps, lab, table, gram_acc = take(8)
    stage = take(4)
    nb_ref, coef_ref, cross_ref, block_ref = stage
    ssend, p, up, below, above = each(), each(), each(), each(), each()
    uown, urecv = [each(), each()], [each(), each()]
    acc, t_acc, t_send, t_recv, op_hi, op_lo, m_acc = (each() for _ in range(7))
    ct = [each(), each()]
    (loc, out_s, s_s, s_r, bm_s, bm_r, u_s, u_r, h_s, h_r, t_s, t_r, n_s, n_r, meet) = take(15)

    g = lax.axis_index("grid")
    d = lax.axis_index("cols")
    chip, core = d // 2, lax.rem(d, 2)
    me = 2 * g + core
    mate = (g, 2 * chip + 1 - core)
    far = [lax.rem(chip + k, chips) for k in range(1, chips)]
    same = [(g, 2 * y + core) for y in far]
    cross = [(g, 2 * y + 1 - core) for y in far]

    def line(q):
        return (q // 2, 2 * chip + lax.rem(q, 2))

    def slab(q):
        return (q, d)

    c_sums = [[Reduction(take(4), n16, me, line) for _ in batches] for _ in range(2)]
    t_sums = [Reduction(take(4), grid_size, g, slab) for _ in batches]
    g_sum = Reduction(take(4), n16, me, line)
    m_sum = Reduction(take(4), n16, me, line)

    partners = [
        line(me + (1 << i) * (1 - 2 * lax.rem(me // (1 << i), 2))) for i in range(bits)
    ]
    barrier = pltpu.get_barrier_semaphore()
    for peer in same + cross + partners:
        pl.semaphore_signal(barrier, inc=1, device_id=peer, device_id_type=MESH)

    def meet_signal(i):
        if i < bits:
            pl.semaphore_signal(meet.at[i], inc=1, device_id=partners[i], device_id_type=MESH)

    def meet_wait(i):
        if i < bits:
            pl.semaphore_wait(meet.at[i], 1)

    loads = [
        pltpu.make_async_copy(src, dst, loc.at[i])
        for i, (src, dst) in enumerate(
            [(s_ref, sland), (b_ref, bland), (eps_ref, eps), (lab_ref, lab), (sig_ref, table)]
        )
    ]
    for load in loads:
        load.start()

    for b in batches:
        zero = jnp.zeros((3, q_rows[b], LANES), F32)
        for edge in (0, tiles + 1):
            p[b][edge] = zero
        above[b][0] = zero[:2]

        @pl.when(me == 0)
        def _():
            below[b][...] = jnp.zeros(below[b].shape, F32)

        @pl.when(me == n16 - 1)
        def _():
            above[b][...] = jnp.zeros(above[b].shape, F32)

    def mine_of(first, second):
        return jnp.where(core == 0, first, second), jnp.where(core == 0, second, first)

    loads[0].wait()

    def my_cols(b):
        return pl.ds(pl.multiple_of(d * widths[b], SUBS), widths[b])

    for b in batches:

        def sort_s(t, carry):
            for a in range(3):
                layers = []
                for layer in range(2):
                    start = starts[b] * per_col + (2 * tiles * a + layer) + 2 * t
                    layers.append(sland[pl.ds(start, widths[b], stride=per_col), :])
                own, other = mine_of(*layers)
                p[b][t + 1, a, my_cols(b), :] = own
                ssend[b][t, a] = other
            return carry

        lax.fori_loop(0, tiles, sort_s, 0)

    pl.semaphore_wait(barrier, 2 * (chips - 1) + bits)
    s_copies = []
    for b in batches:
        landing = p[b].at[pl.ds(1, tiles), :, my_cols(b), :]
        plan = [(landing, peer) for peer in same]
        plan += [(ssend[b], peer) for peer in cross + [mate]]
        for i, (src, peer) in enumerate(plan):
            copy = remote(src, landing, s_s.at[b, i], s_r.at[b, i], peer)
            copy.start()
            s_copies.append((b, copy))
    meet_signal(0)

    def b_rows(which):
        return pl.ds(pl.multiple_of(which * own_b, own_b), own_b)

    def put_b(t, a, which, value):
        high, low = split(value)
        lanes = pl.ds(pl.multiple_of((lax.rem(t, CHUNK) * 3 + a) * LANES, LANES), LANES)
        bhi[t // CHUNK, b_rows(which), lanes] = high
        blo[t // CHUNK, b_rows(which), lanes] = low

    def sort_b(t, carry):
        for a in range(3):
            layers = []
            for layer in range(2):
                start = (2 * tiles * a + layer) + 2 * t
                layers.append(bland[pl.ds(start, own_b, stride=per_col), :])
            own, other = mine_of(*layers)
            bsend[t, a] = other
            put_b(t, a, core, own)
        remote(bsend.at[t], brecv.at[t], bm_s.at[t], bm_r.at[t], mate).start()
        return carry

    loads[1].wait()
    lax.fori_loop(0, tiles, sort_b, 0)
    meet_wait(0)
    meet_signal(1)

    def mate_b(t, carry):
        remote(bsend.at[t], brecv.at[t], bm_s.at[t], bm_r.at[t], mate).wait()
        for a in range(3):
            put_b(t, a, 1 - core, brecv[t, a])
        return carry

    lax.fori_loop(0, tiles // 2, mate_b, 0)
    meet_wait(1)
    meet_signal(2)
    lax.fori_loop(tiles // 2, tiles, mate_b, 0)
    meet_wait(2)
    meet_signal(3)

    for load in loads[2:]:
        load.wait()
    region = lab[...]
    picked = jnp.zeros(region.shape, F32)
    for k in range(sig_ref.shape[0]):
        picked = jnp.where(region == k, table[k], picked)
    sig[...] = picked

    def field_chunk(buffer, j):
        parts = [buffer[CHUNK * j + i // 3 + 1, i % 3] for i in range(3 * CHUNK)]
        return jnp.concatenate(parts, axis=1)

    per_row = chip_b // LANES

    def put_coef(total, sweep, b):
        work = c_sums[sweep][b]
        for i in range(q_rows[b] // SUBS):
            for k in range(per_row):
                work.put(
                    i * per_row + k,
                    total[SUBS * i : SUBS * (i + 1), LANES * k : LANES * (k + 1)],
                )
        work.scatter()

    def get_coef(sweep, b):
        work = c_sums[sweep][b]
        work.finish()
        rows = []
        for i in range(q_rows[b] // SUBS):
            rows.append(
                jnp.concatenate([work.get(i * per_row + k) for k in range(per_row)], axis=1)
            )
        ct[sweep][b][...] = jnp.concatenate(rows, axis=0)

    def descending(body, count=chunks):
        def step(i, carry):
            body(chunks - 1 - i)
            return carry

        lax.fori_loop(0, count, step, 0)

    def first_coef(b):
        acc[b][...] = jnp.zeros_like(acc[b])

        def body(j):
            acc[b][...] += exact_dot(dot_nt, field_chunk(p[b], j), (bhi[j], blo[j]))

        descending(body)
        put_coef(acc[b][...], 0, b)

    def u_copy(sweep, b, j, k):
        part = pl.ds(CHUNK * j, CHUNK)
        return remote(
            uown[sweep][b].at[part],
            urecv[sweep][b].at[k, part],
            u_s.at[sweep, b, k, j],
            u_r.at[sweep, b, k, j],
            same[k],
        )

    def combine(sweep, b):
        weights = ct[sweep][b][...]

        def body(j):
            u = exact_dot(dot_nn, weights, (bhi[j], blo[j]))
            for i in range(3 * CHUNK):
                uown[sweep][b][CHUNK * j + i // 3, i % 3] = u[:, LANES * i : LANES * (i + 1)]
            for k in range(chips - 1):
                u_copy(sweep, b, j, k).start()

        descending(body)

    def remove(sweep, b, j):
        for k in range(chips - 1):
            u_copy(sweep, b, j, k).wait()
        parts = []
        for i in range(3 * CHUNK):
            t, a = CHUNK * j + i // 3, i % 3
            total = uown[sweep][b][t, a]
            for k in range(chips - 1):
                total = total + urecv[sweep][b][k, t, a]
            left = p[b][t + 1, a] - total
            p[b][t + 1, a] = left
            parts.append(left)
        return parts

    def second_coef(b):
        acc[b][...] = jnp.zeros_like(acc[b])

        def body(j):
            field = jnp.concatenate(remove(0, b, j), axis=1)
            acc[b][...] += exact_dot(dot_nt, field, (bhi[j], blo[j]))

        descending(body)
        put_coef(acc[b][...], 1, b)

    lane = lax.broadcasted_iota(jnp.int32, (max(q_rows), LANES), 1)
    y_at = lax.rem(lane, NY)
    y_top, y_low = y_at != NY - 1, y_at != 0
    x_low, x_top = lane < NY, lane >= LANES - NY

    def yp(f):
        return jnp.where(y_top[: f.shape[0]], pltpu.roll(f, LANES - 1, 1), 0.0)

    def ym(f):
        return jnp.where(y_low[: f.shape[0]], pltpu.roll(f, 1, 1), 0.0)

    def xp(f, after):
        return pltpu.roll(jnp.where(x_low[: f.shape[0]], after, f), LANES - NY, 1)

    def xm(f, before):
        return pltpu.roll(jnp.where(x_top[: f.shape[0]], before, f), NY, 1)

    def halo(b, j, to_next):
        part = pl.ds(CHUNK * j, CHUNK)
        shifted = pl.ds(CHUNK * j + 1, CHUNK)
        if to_next:
            src, dst = up[b].at[part], below[b].at[part]
        else:
            src, dst = p[b].at[shifted, pl.ds(0, 2)], above[b].at[shifted]
        at = 0 if to_next else 1
        return remote(
            src, dst, h_s.at[b, at, j], h_r.at[b, at, j], line(me + 1 if to_next else me - 1)
        )

    def finish_field(b, j):
        remove(1, b, j)

        @pl.when(me > 0)
        def _():
            halo(b, j, False).start()

        for c in range(CHUNK):
            t = CHUNK * j + c
            ex, ey, ez = (p[b][t + 1, a] for a in range(3))
            up[b][t, 0] = ex + xp(ez, p[b][t + 2, 2]) - ez
            up[b][t, 1] = ey + yp(ez) - ez

        @pl.when(me < n16 - 1)
        def _():
            halo(b, j, True).start()

    def halo_wait(b, j):
        @pl.when(me > 0)
        def _():
            halo(b, j, True).wait_recv()
            halo(b, j, False).wait_send()

        @pl.when(me < n16 - 1)
        def _():
            halo(b, j, False).wait_recv()
            halo(b, j, True).wait_send()

    def curl_tile(b, t):
        at = t + 1
        ex, ey, ez = (p[b][at, a] for a in range(3))
        ex_b, ey_b, ez_b = (p[b][at - 1, a] for a in range(3))
        ey_x = xp(ey, p[b][at + 1, 1])
        ez_x = xp(ez, p[b][at + 1, 2])
        ux, uy = above[b][at, 0], above[b][at, 1]
        v = ey_x - ey
        image_x = 4.0 * ex - yp(ex) - ym(ex + v) + v - ux - below[b][t, 0] + ez_x - ez
        h = ex - xm(ex, ex_b) + ez
        image_y = 4.0 * ey - ey_x - xm(ey, ey_b) - uy - below[b][t, 1] + yp(h) - h
        du = ux - ex
        du_b = above[b][at - 1, 0] - ex_b
        dv = uy - ey
        image_z = (
            4.0 * ez - ez_x - yp(ez) - xm(ez + du, ez_b + du_b) - ym(ez + dv) + du + dv
        )
        return [image_x, image_y, image_z]

    def layer_row(ref, row):
        return jnp.where(core == 0, ref[pl.ds(row, 1), :], ref[pl.ds(row + 1, 1), :])

    def operators(b, j):
        images = [[], [], []]
        for c in range(CHUNK):
            t = CHUNK * j + c
            images[0] += curl_tile(b, t)
            loss = layer_row(sig, 2 * t)
            for a in range(3):
                field = p[b][t + 1, a]
                images[1].append(field * layer_row(eps, 2 * tiles * a + 2 * t))
                images[2].append(field * loss)
        stack = jnp.concatenate([jnp.concatenate(i, axis=1) for i in images], axis=0)
        high, low = split(stack)
        op_hi[b][j] = high
        op_lo[b][j] = low
        t_acc[b][...] += dot_nt(high, bhi[j]) + dot_nt(high, blo[j]) + dot_nt(low, bhi[j])

    def lagged(b, j):
        halo_wait(b, j - 1)
        operators(b, j)

    def all_operators(b):
        halo_wait(b, chunks - 1)
        descending(functools.partial(lagged, b), chunks - 1)
        operators(b, 0)

    def t_copy(b):
        return remote(t_send[b], t_recv[b], t_s.at[b], t_r.at[b], mate)

    def t_start(b):
        for k in range(3):
            total = t_acc[b][q_rows[b] * k : q_rows[b] * (k + 1)]
            t_send[b][k] = jnp.where(core == 0, total[:, own_b:], total[:, :own_b])
        t_copy(b).start()

    per_own = own_b // LANES

    def t_scatter(b):
        t_copy(b).wait()
        blocks = q_rows[b] // SUBS
        for k in range(3):
            total = t_acc[b][q_rows[b] * k : q_rows[b] * (k + 1)]
            mine = jnp.where(core == 0, total[:, :own_b], total[:, own_b:]) + t_recv[b][k]
            for i in range(blocks):
                for c in range(per_own):
                    t_sums[b].put(
                        (k * blocks + i) * per_own + c,
                        mine[SUBS * i : SUBS * (i + 1), LANES * c : LANES * (c + 1)],
                    )
        t_sums[b].scatter()

    def t_rows(b, k):
        blocks = q_rows[b] // SUBS
        rows = []
        for i in range(blocks):
            at = (k * blocks + i) * per_own
            rows.append(
                jnp.concatenate([t_sums[b].get(at + c) for c in range(per_own)], axis=1)
            )
        return jnp.concatenate(rows, axis=0)

    def in_order(parts):
        rows = []
        for e in range(cols):
            for b in batches:
                rows.append(parts[b][widths[b] * e : widths[b] * (e + 1)])
        return jnp.concatenate(rows, axis=0)

    def gram_chunk(j):
        high, low = split(in_order([field_chunk(p[b], j) for b in batches]))
        p2_hi[j] = high
        p2_lo[j] = low
        gram_acc[...] += dot_nt(high, high) + dot_nt(high, low) + dot_nt(low, high)

    def s_wait(b):
        for at, copy in s_copies:
            if at == b:
                copy.wait()

    writes = {}

    def write(i):
        writes[i] = pltpu.make_async_copy(stage[i], outs[i], out_s.at[i])
        writes[i].start()

    for b in batches:
        s_wait(b)
        if b == 0:
            meet_wait(3)
            for i in range(4, bits):
                meet_signal(i)
                meet_wait(i)
        first_coef(b)
        if b:
            get_coef(0, b - 1)
            combine(0, b - 1)
        c_sums[0][b].spread()
    second_coef(0)
    get_coef(0, last)
    combine(0, last)
    c_sums[1][0].spread()
    get_coef(1, 0)
    combine(1, 0)
    for b in batches[1:]:
        second_coef(b)
        if b > 1:
            get_coef(1, b - 1)
            combine(1, b - 1)
        c_sums[1][b].spread()
    for b in batches:
        t_acc[b][...] = jnp.zeros_like(t_acc[b])
        m_acc[b][...] = jnp.zeros_like(m_acc[b])
    gram_acc[...] = jnp.zeros_like(gram_acc)
    descending(functools.partial(finish_field, 0))
    get_coef(1, last)
    combine(1, last)

    coef_t[...] = in_order([ct[0][b][...] + ct[1][b][...] for b in batches])
    coef_ref[...] = jnp.where(core == 0, coef_t[:, :own_b], coef_t[:, own_b:]).T
    write(1)

    for b in batches[:-1]:
        then = b + 1
        if then != last:
            finish_field(then, chunks - 1)
            all_operators(b)
            t_start(b)
            for j in reversed(range(chunks - 1)):
                finish_field(then, j)
                if j == chunks - 2:
                    t_scatter(b)
                if j == 1:
                    t_sums[b].spread()
        else:

            halo_wait(b, chunks - 1)

            def both(j):
                lagged(b, j)
                finish_field(then, j)
                gram_chunk(j)

            descending(both, chunks - 1)
            operators(b, 0)
            t_start(b)
            finish_field(then, 0)
            gram_chunk(0)
    for i in range(total_s // SUBS):
        g_sum.put(i, gram_acc[SUBS * i : SUBS * (i + 1), :])
    g_sum.scatter()
    t_scatter(last - 1)

    halo_wait(last, chunks - 1)
    descending(functools.partial(lagged, last), chunks - 1)
    g_sum.spread()
    operators(last, 0)
    t_start(last)

    def m_chunk(j):
        high, low = p2_hi[j], p2_lo[j]
        for b in batches:
            m_acc[b][...] += (
                dot_nt(op_hi[b][j], high) + dot_nt(op_hi[b][j], low) + dot_nt(op_lo[b][j], high)
            )

    descending(m_chunk)
    t_scatter(last)
    row_blocks = total_s // SUBS
    for k in range(3):
        rows = in_order([m_acc[b][q_rows[b] * k : q_rows[b] * (k + 1)] for b in batches])
        for i in range(row_blocks):
            m_sum.put(k * row_blocks + i, rows[SUBS * i : SUBS * (i + 1)])
    m_sum.scatter()
    t_sums[last - 1].spread()
    g_sum.finish()

    def between():
        t_sums[last].spread()
        m_sum.spread()

    gram_rows = [g_sum.get(i) * (1.0 / unknowns) for i in range(row_blocks)]
    for i, value in enumerate(inverse_factor(gram_rows, between)):
        inv_ref[SUBS * i : SUBS * (i + 1)] = value

    def own_rows(which):
        return pl.ds(pl.multiple_of(which * own_s, SUBS), own_s)

    inv_own = inv_ref[own_rows(d), :]
    inv_mate = inv_ref[own_rows(2 * chip + 1 - core), :]
    inv_chip = jnp.concatenate([inv_own, inv_mate], axis=0)

    def nb_copy(j):
        part = pl.ds(CHUNK * j, CHUNK)
        return remote(nb_send.at[part], nb_recv.at[part], n_s.at[j], n_r.at[j], mate)

    def nb_body(j):
        value = exact_dot(dot_nn, inv_chip, (p2_hi[j], p2_lo[j]))
        for i in range(3 * CHUNK):
            t, a = CHUNK * j + i // 3, i % 3
            part = value[:, LANES * i : LANES * (i + 1)]
            nb_own[t, a] = part[:own_s]
            nb_send[t, a] = part[own_s:]
        nb_copy(j).start()

    descending(nb_body)
    inverse = inv_ref[...]
    inverse_halves = split(inverse)
    for b in batches:
        t_sums[b].finish()
    for k in range(3):
        cross_ref[k] = exact_dot(dot_nn, inverse, in_order([t_rows(b, k) for b in batches])).T
    write(2)

    def nb_out(j):
        nb_copy(j).wait()
        for i in range(3 * CHUNK):
            t, a = CHUNK * j + i // 3, i % 3
            layers = mine_of(nb_own[t, a], nb_recv[t, a])
            for layer in range(2):
                start = (2 * tiles * a + layer) + 2 * t
                nb_ref[pl.ds(start, own_s, stride=per_col), :] = layers[layer]

    descending(nb_out)
    write(0)
    m_sum.finish()
    for k in range(3):
        rows = [m_sum.get(k * row_blocks + i) for i in range(row_blocks)]
        half = exact_dot(dot_nn, inv_own, jnp.concatenate(rows, axis=0))
        block_ref[k] = exact_dot(dot_nt, half, inverse_halves) * (1.0 / unknowns)
    write(3)
    for copy in writes.values():
        copy.wait()


def hand_over(*refs):
    sources, targets, held, sems = refs[:4], refs[4:8], refs[8:12], refs[12]
    reads = [pltpu.make_async_copy(sources[i], held[i], sems.at[0, i]) for i in range(4)]
    writes = [pltpu.make_async_copy(held[i], targets[i], sems.at[1, i]) for i in range(4)]
    for copy in reads:
        copy.start()
    for read, copy in zip(reads, writes):
        read.wait()
        copy.start()
    for copy in writes:
        copy.wait()


def shards(basis, snapshots, permittivity, labels, sigma_table):
    own_b, own_s = basis.shape[0], snapshots.shape[0]
    layers, layer = basis.shape[2:]
    assert layers == 2
    grid_size, cols = lax.axis_size("grid"), lax.axis_size("cols")
    tiles = layer // LANES
    chips = cols // 2
    n16 = 2 * grid_size
    widths = batch_widths(own_s)
    q_rows = [width * cols for width in widths]
    total_s = own_s * cols
    chip_b = 2 * own_b
    chunks = tiles // CHUNK
    depth = CHUNK * 3 * LANES
    per_col = 6 * tiles
    count = len(widths)

    def rows_of(value):
        lead = value.shape[:-2]
        value = value.reshape(lead + (layers, tiles, LANES))
        return jnp.swapaxes(value, -3, -2).reshape(-1, LANES)

    def vmem(*shape, dtype=F32):
        return pltpu.VMEM(shape, dtype)

    out_shapes = [
        (own_s * per_col, LANES),
        (own_b, total_s),
        (3, own_b, total_s),
        (3, own_s, total_s),
    ]
    scratch = [
        vmem(own_s * per_col, LANES),
        vmem(own_b * per_col, LANES),
        vmem(tiles, 3, own_b, LANES),
        vmem(tiles, 3, own_b, LANES),
        vmem(chunks, chip_b, depth, dtype=BF16),
        vmem(chunks, chip_b, depth, dtype=BF16),
        vmem(chunks, total_s, depth, dtype=BF16),
        vmem(chunks, total_s, depth, dtype=BF16),
        vmem(total_s, chip_b),
        vmem(total_s, total_s),
    ]
    scratch += [vmem(tiles, 3, own_s, LANES)] * 3
    scratch += [vmem(layers * tiles, LANES), vmem(3 * layers * tiles, LANES)]
    scratch += [vmem(layers * tiles, LANES, dtype=labels.dtype)]
    scratch += [pltpu.SMEM(sigma_table.shape, F32), vmem(total_s, total_s)]
    scratch += [vmem(*shape) for shape in out_shapes]
    scratch += [vmem(tiles, 3, width, LANES) for width in widths]
    scratch += [vmem(tiles + 2, 3, q, LANES) for q in q_rows]
    scratch += [vmem(tiles, 2, q, LANES) for q in q_rows] * 2
    scratch += [vmem(tiles + 1, 2, q, LANES) for q in q_rows]
    scratch += [vmem(tiles, 3, q, LANES) for q in q_rows] * 2
    scratch += [vmem(chips - 1, tiles, 3, q, LANES) for q in q_rows] * 2
    scratch += [vmem(q, chip_b) for q in q_rows]
    scratch += [vmem(3 * q, chip_b) for q in q_rows]
    scratch += [vmem(3, q, own_b) for q in q_rows] * 2
    scratch += [vmem(chunks, 3 * q, depth, dtype=BF16) for q in q_rows] * 2
    scratch += [vmem(3 * q, total_s) for q in q_rows]
    scratch += [vmem(q, chip_b) for q in q_rows] * 2
    sem = pltpu.SemaphoreType.DMA
    scratch += [sem((5,)), sem((4,))]
    scratch += [sem((count, 2 * chips - 1))] * 2
    scratch += [sem((tiles,))] * 2
    scratch += [sem((2, count, chips - 1, chunks))] * 2
    scratch += [sem((count, 2, chunks))] * 2
    scratch += [sem((count,))] * 2
    scratch += [sem((chunks,))] * 2
    scratch += [pltpu.SemaphoreType.REGULAR((log2(n16),))]
    vreg = SUBS * LANES
    for _ in range(2):
        for q in q_rows:
            scratch += reduction_scratch(n16, q * chip_b // vreg)
    for q in q_rows:
        scratch += reduction_scratch(grid_size, 3 * q * own_b // vreg)
    scratch += reduction_scratch(n16, total_s * total_s // vreg)
    scratch += reduction_scratch(n16, 3 * total_s * total_s // vreg)

    anywhere = pl.BlockSpec(memory_space=pl.ANY)
    outputs = [jax.ShapeDtypeStruct(shape, F32) for shape in out_shapes]
    dims = (grid_size, cols, own_b, own_s, tiles)
    results = pl.pallas_call(
        functools.partial(kernel, dims),
        out_shape=outputs,
        in_specs=[anywhere] * 5,
        out_specs=[anywhere] * 4,
        scratch_shapes=scratch,
        compiler_params=pltpu.CompilerParams(
            collective_id=0, has_side_effects=True, vmem_limit_bytes=62 << 20
        ),
    )(
        rows_of(basis),
        rows_of(snapshots),
        rows_of(permittivity),
        rows_of(labels),
        sigma_table,
    )
    new_rows, coefficients, cross_terms, block_terms = pl.pallas_call(
        hand_over,
        out_shape=outputs,
        in_specs=[anywhere] * 4,
        out_specs=[anywhere] * 4,
        scratch_shapes=[vmem(*shape) for shape in out_shapes] + [sem((2, 4))],
    )(*results)
    new_basis = jnp.swapaxes(
        new_rows.reshape(own_s, 3, tiles, layers, LANES), 2, 3
    ).reshape(snapshots.shape)
    return (new_basis, coefficients, cross_terms, block_terms)


def solution(mesh):
    placed = (
        P("cols", None, "grid", None),
        P("cols", None, "grid", None),
        P(None, "grid", None),
        P("grid", None),
        P(),
    )
    return jax.shard_map(
        shards,
        mesh=mesh,
        in_specs=placed,
        out_specs=(
            P("cols", None, "grid", None),
            P("cols", None),
            P(None, "cols", None),
            P(None, "cols", None),
        ),
        check_vma=False,
    )
```

```python
import functools

import jax
import jax.numpy as jnp
from jax import lax
from jax.experimental import pallas as pl
from jax.experimental.pallas import tpu as pltpu
from jax.sharding import PartitionSpec as P

NY = 32
LANES = 128
SUBS = 8
CHUNK = 2
PIVOTS = 4
MESH = pl.DeviceIdType.MESH
F32 = jnp.float32
BF16 = jnp.bfloat16


def split(value):
    high = value.astype(BF16)
    return high, (value - high.astype(F32)).astype(BF16)


def dot_nt(left, right):
    return lax.dot_general(
        left, right, (((1,), (1,)), ((), ())), preferred_element_type=F32
    )


def dot_nn(left, right):
    return lax.dot_general(
        left, right, (((1,), (0,)), ((), ())), preferred_element_type=F32
    )


def exact_dot(dot, left, right):
    rows = left.shape[0]
    stacked = jnp.concatenate(split(left), axis=0)
    high, low = right if isinstance(right, tuple) else split(right)
    total = dot(stacked, high) + dot(stacked, low)
    return total[:rows] + total[rows:]


def inverse_factor(rows, between):
    count = len(rows)
    size = count * SUBS
    shape = (SUBS, size)
    left = list(rows)
    lane = lax.broadcasted_iota(jnp.int32, shape, 1)
    sub = lax.broadcasted_iota(jnp.int32, shape, 0)
    right = [jnp.where(lane == sub + SUBS * i, 1.0, 0.0).astype(F32) for i in range(count)]

    def spread(value):
        return jnp.broadcast_to(value, shape)

    for k in range(0, size, PIVOTS):
        if k == size // 2:
            between()
        block, first = divmod(k, SUBS)
        row_l = [spread(left[block][first + t : first + t + 1]) for t in range(PIVOTS)]
        row_r = [spread(right[block][first + t : first + t + 1]) for t in range(PIVOTS)]
        pivot = {
            (s, t): spread(row_l[s][:, k + t : k + t + 1])
            for s in range(PIVOTS)
            for t in range(s + 1)
        }
        scale, factor = [], {}
        for t in range(PIVOTS):
            scale.append(lax.rsqrt(pivot[t, t]))
            row_l[t] = row_l[t] * scale[t]
            row_r[t] = row_r[t] * scale[t]
            for s in range(t + 1, PIVOTS):
                factor[s, t] = pivot[s, t] * scale[t]
            for s in range(t + 1, PIVOTS):
                for u in range(t + 1, s + 1):
                    pivot[s, u] = pivot[s, u] - factor[s, t] * factor[u, t]
                row_l[s] = row_l[s] - factor[s, t] * row_l[t]
                row_r[s] = row_r[s] - factor[s, t] * row_r[t]
        for at in range(block, count):
            inside = at == block
            if not inside or first + PIVOTS < SUBS:
                cols = [spread(left[at][:, k + t : k + t + 1]) for t in range(PIVOTS)]
                for t in range(PIVOTS):
                    cols[t] = cols[t] * scale[t]
                    for s in range(t + 1, PIVOTS):
                        cols[s] = cols[s] - factor[s, t] * cols[t]
                if inside:
                    cols = [jnp.where(sub >= first + PIVOTS, c, 0.0) for c in cols]
                for t in range(PIVOTS):
                    left[at] = left[at] - cols[t] * row_l[t]
                    right[at] = right[at] - cols[t] * row_r[t]
            if inside:
                for t in range(PIVOTS):
                    right[at] = jnp.where(sub == first + t, row_r[t], right[at])
    return right


def remote(src, dst, send_sem, recv_sem, peer):
    return pltpu.make_async_remote_copy(
        src_ref=src,
        dst_ref=dst,
        send_sem=send_sem,
        recv_sem=recv_sem,
        device_id=peer,
        device_id_type=MESH,
    )


class Reduction:
    def __init__(self, refs, n, me, peer):
        self.x, self.slots, self.o, self.sems = refs
        self.n, self.me, self.peer = n, me, peer

    def put(self, at, value):
        blocks = self.x.shape[1]
        self.x[at // blocks, at % blocks] = value

    def get(self, at):
        blocks = self.x.shape[1]
        return self.o[at // blocks, at % blocks]

    def scatter(self):
        def body(k, carry):
            q = lax.rem(self.me + k, self.n)
            remote(
                self.x.at[q], self.slots.at[k - 1], self.sems.at[0], self.sems.at[1], self.peer(q)
            ).start()
            return carry

        lax.fori_loop(1, self.n, body, 0)

    def spread(self):
        whole = remote(self.slots, self.slots, self.sems.at[0], self.sems.at[1], self.peer(self.me))
        whole.wait_recv()
        self.o[self.me] = self.x[self.me] + jnp.sum(self.slots[...], axis=0)

        def body(k, carry):
            q = lax.rem(self.me + k, self.n)
            mine = self.o.at[self.me]
            remote(mine, mine, self.sems.at[2], self.sems.at[3], self.peer(q)).start()
            return carry

        lax.fori_loop(1, self.n, body, 0)
        whole.wait_send()

    def finish(self):
        rest = self.o.at[pl.ds(0, self.n - 1)]
        whole = remote(rest, rest, self.sems.at[2], self.sems.at[3], self.peer(self.me))
        whole.wait_recv()
        whole.wait_send()


def reduction_scratch(n, blocks):
    piece = -(-blocks // n)
    shapes = [(n, piece), (n - 1, piece), (n, piece)]
    return [pltpu.VMEM(s + (SUBS, LANES), F32) for s in shapes] + [pltpu.SemaphoreType.DMA((4,))]


def batch_widths(own_s):
    if own_s % (4 * SUBS) == 0:
        return (own_s // 4, own_s // 2, own_s // 4)
    return (own_s // 2, own_s // 2)


def log2(n):
    bits = n.bit_length() - 1
    assert n == 1 << bits
    return bits


def kernel(dims, b_ref, s_ref, eps_ref, lab_ref, sig_ref, *rest):
    (grid_size, cols, own_b, own_s, tiles) = dims
    chips = cols // 2
    n16 = 2 * grid_size
    bits = log2(n16)
    widths = batch_widths(own_s)
    starts = [sum(widths[:b]) for b in range(len(widths))]
    batches = range(len(widths))
    last = len(widths) - 1
    q_rows = [width * cols for width in widths]
    total_s = own_s * cols
    chip_b = 2 * own_b
    chunks = tiles // CHUNK
    per_col = 6 * tiles
    unknowns = 3 * tiles * LANES * n16

    outs = rest[:4]
    refs = list(rest[4:])

    def take(count):
        out = refs[:count]
        del refs[:count]
        return out

    def each():
        return take(len(widths))

    sland, bland, bsend, brecv, bhi, blo, p2_hi, p2_lo, coef_t, inv_ref = take(10)
    nb_own, nb_send, nb_recv, sig, eps, lab, table, gram_acc = take(8)
    stage = take(4)
    nb_ref, coef_ref, cross_ref, block_ref = stage
    ssend, p, up, below, above = each(), each(), each(), each(), each()
    uown, urecv = [each(), each()], [each(), each()]
    acc, t_acc, t_send, t_recv, op_hi, op_lo, m_acc = (each() for _ in range(7))
    ct = [each(), each()]
    (loc, out_s, s_s, s_r, bm_s, bm_r, u_s, u_r, h_s, h_r, t_s, t_r, n_s, n_r, meet) = take(15)

    g = lax.axis_index("grid")
    d = lax.axis_index("cols")
    chip, core = d // 2, lax.rem(d, 2)
    me = 2 * g + core
    mate = (g, 2 * chip + 1 - core)
    far = [lax.rem(chip + k, chips) for k in range(1, chips)]
    same = [(g, 2 * y + core) for y in far]
    cross = [(g, 2 * y + 1 - core) for y in far]

    def line(q):
        return (q // 2, 2 * chip + lax.rem(q, 2))

    def slab(q):
        return (q, d)

    c_sums = [[Reduction(take(4), n16, me, line) for _ in batches] for _ in range(2)]
    t_sums = [Reduction(take(4), grid_size, g, slab) for _ in batches]
    g_sum = Reduction(take(4), n16, me, line)
    m_sum = Reduction(take(4), grid_size, g, slab)
    m_send, m_recv, m_got, m_sems = take(4)

    partners = [
        line(me + (1 << i) * (1 - 2 * lax.rem(me // (1 << i), 2))) for i in range(bits)
    ]
    barrier = pltpu.get_barrier_semaphore()
    for peer in same + cross + partners:
        pl.semaphore_signal(barrier, inc=1, device_id=peer, device_id_type=MESH)

    def meet_signal(i):
        if i < bits:
            pl.semaphore_signal(meet.at[i], inc=1, device_id=partners[i], device_id_type=MESH)

    def meet_wait(i):
        if i < bits:
            pl.semaphore_wait(meet.at[i], 1)

    loads = [
        pltpu.make_async_copy(src, dst, loc.at[i])
        for i, (src, dst) in enumerate(
            [(s_ref, sland), (b_ref, bland), (eps_ref, eps), (lab_ref, lab), (sig_ref, table)]
        )
    ]
    for load in loads:
        load.start()

    for b in batches:
        zero = jnp.zeros((3, q_rows[b], LANES), F32)
        for edge in (0, tiles + 1):
            p[b][edge] = zero
        above[b][0] = zero[:2]

        @pl.when(me == 0)
        def _():
            below[b][...] = jnp.zeros(below[b].shape, F32)

        @pl.when(me == n16 - 1)
        def _():
            above[b][...] = jnp.zeros(above[b].shape, F32)

    def mine_of(first, second):
        return jnp.where(core == 0, first, second), jnp.where(core == 0, second, first)

    loads[0].wait()

    def my_cols(b):
        return pl.ds(pl.multiple_of(d * widths[b], SUBS), widths[b])

    for b in batches:

        def sort_s(t, carry):
            for a in range(3):
                layers = []
                for layer in range(2):
                    start = starts[b] * per_col + (2 * tiles * a + layer) + 2 * t
                    layers.append(sland[pl.ds(start, widths[b], stride=per_col), :])
                own, other = mine_of(*layers)
                p[b][t + 1, a, my_cols(b), :] = own
                ssend[b][t, a] = other
            return carry

        lax.fori_loop(0, tiles, sort_s, 0)

    pl.semaphore_wait(barrier, 2 * (chips - 1) + bits)
    s_copies = []
    for b in batches:
        landing = p[b].at[pl.ds(1, tiles), :, my_cols(b), :]
        plan = [(landing, peer) for peer in same]
        plan += [(ssend[b], peer) for peer in cross + [mate]]
        for i, (src, peer) in enumerate(plan):
            copy = remote(src, landing, s_s.at[b, i], s_r.at[b, i], peer)
            copy.start()
            s_copies.append((b, copy))
    meet_signal(0)

    def b_rows(which):
        return pl.ds(pl.multiple_of(which * own_b, own_b), own_b)

    def put_b(t, a, which, value):
        high, low = split(value)
        lanes = pl.ds(pl.multiple_of((lax.rem(t, CHUNK) * 3 + a) * LANES, LANES), LANES)
        bhi[t // CHUNK, b_rows(which), lanes] = high
        blo[t // CHUNK, b_rows(which), lanes] = low

    def sort_b(t, carry):
        for a in range(3):
            layers = []
            for layer in range(2):
                start = (2 * tiles * a + layer) + 2 * t
                layers.append(bland[pl.ds(start, own_b, stride=per_col), :])
            own, other = mine_of(*layers)
            bsend[t, a] = other
            put_b(t, a, core, own)
        remote(bsend.at[t], brecv.at[t], bm_s.at[t], bm_r.at[t], mate).start()
        return carry

    loads[1].wait()
    lax.fori_loop(0, tiles, sort_b, 0)
    meet_wait(0)
    meet_signal(1)

    def mate_b(t, carry):
        remote(bsend.at[t], brecv.at[t], bm_s.at[t], bm_r.at[t], mate).wait()
        for a in range(3):
            put_b(t, a, 1 - core, brecv[t, a])
        return carry

    lax.fori_loop(0, tiles // 2, mate_b, 0)
    meet_wait(1)
    meet_signal(2)
    lax.fori_loop(tiles // 2, tiles, mate_b, 0)
    meet_wait(2)
    meet_signal(3)

    for load in loads[2:]:
        load.wait()
    region = lab[...]
    picked = jnp.zeros(region.shape, F32)
    for k in range(sig_ref.shape[0]):
        picked = jnp.where(region == k, table[k], picked)
    sig[...] = picked

    def field_chunk(buffer, j):
        parts = [buffer[CHUNK * j + i // 3 + 1, i % 3] for i in range(3 * CHUNK)]
        return jnp.concatenate(parts, axis=1)

    per_row = chip_b // LANES

    def put_coef(total, sweep, b):
        work = c_sums[sweep][b]
        for i in range(q_rows[b] // SUBS):
            for k in range(per_row):
                work.put(
                    i * per_row + k,
                    total[SUBS * i : SUBS * (i + 1), LANES * k : LANES * (k + 1)],
                )
        work.scatter()

    def get_coef(sweep, b):
        work = c_sums[sweep][b]
        work.finish()
        rows = []
        for i in range(q_rows[b] // SUBS):
            rows.append(
                jnp.concatenate([work.get(i * per_row + k) for k in range(per_row)], axis=1)
            )
        ct[sweep][b][...] = jnp.concatenate(rows, axis=0)

    def descending(body, count=chunks):
        def step(i, carry):
            body(chunks - 1 - i)
            return carry

        lax.fori_loop(0, count, step, 0)

    def first_coef(b):
        acc[b][...] = jnp.zeros_like(acc[b])

        def body(j):
            acc[b][...] += exact_dot(dot_nt, field_chunk(p[b], j), (bhi[j], blo[j]))

        descending(body)
        put_coef(acc[b][...], 0, b)

    def u_copy(sweep, b, j, k):
        part = pl.ds(CHUNK * j, CHUNK)
        return remote(
            uown[sweep][b].at[part],
            urecv[sweep][b].at[k, part],
            u_s.at[sweep, b, k, j],
            u_r.at[sweep, b, k, j],
            same[k],
        )

    def combine(sweep, b):
        weights = ct[sweep][b][...]

        def body(j):
            u = exact_dot(dot_nn, weights, (bhi[j], blo[j]))
            for i in range(3 * CHUNK):
                uown[sweep][b][CHUNK * j + i // 3, i % 3] = u[:, LANES * i : LANES * (i + 1)]
            for k in range(chips - 1):
                u_copy(sweep, b, j, k).start()

        descending(body)

    def remove(sweep, b, j):
        for k in range(chips - 1):
            u_copy(sweep, b, j, k).wait()
        parts = []
        for i in range(3 * CHUNK):
            t, a = CHUNK * j + i // 3, i % 3
            total = uown[sweep][b][t, a]
            for k in range(chips - 1):
                total = total + urecv[sweep][b][k, t, a]
            left = p[b][t + 1, a] - total
            p[b][t + 1, a] = left
            parts.append(left)
        return parts

    def second_coef(b):
        acc[b][...] = jnp.zeros_like(acc[b])

        def body(j):
            field = jnp.concatenate(remove(0, b, j), axis=1)
            acc[b][...] += exact_dot(dot_nt, field, (bhi[j], blo[j]))

        descending(body)
        put_coef(acc[b][...], 1, b)

    lane = lax.broadcasted_iota(jnp.int32, (max(q_rows), LANES), 1)
    y_at = lax.rem(lane, NY)
    y_top, y_low = y_at != NY - 1, y_at != 0
    x_low, x_top = lane < NY, lane >= LANES - NY

    def yp(f):
        return jnp.where(y_top[: f.shape[0]], pltpu.roll(f, LANES - 1, 1), 0.0)

    def ym(f):
        return jnp.where(y_low[: f.shape[0]], pltpu.roll(f, 1, 1), 0.0)

    def xp(f, after):
        return pltpu.roll(jnp.where(x_low[: f.shape[0]], after, f), LANES - NY, 1)

    def xm(f, before):
        return pltpu.roll(jnp.where(x_top[: f.shape[0]], before, f), NY, 1)

    def halo(b, j, to_next):
        part = pl.ds(CHUNK * j, CHUNK)
        shifted = pl.ds(CHUNK * j + 1, CHUNK)
        if to_next:
            src, dst = up[b].at[part], below[b].at[part]
        else:
            src, dst = p[b].at[shifted, pl.ds(0, 2)], above[b].at[shifted]
        at = 0 if to_next else 1
        return remote(
            src, dst, h_s.at[b, at, j], h_r.at[b, at, j], line(me + 1 if to_next else me - 1)
        )

    def finish_field(b, j):
        remove(1, b, j)

        @pl.when(me > 0)
        def _():
            halo(b, j, False).start()

        for c in range(CHUNK):
            t = CHUNK * j + c
            ex, ey, ez = (p[b][t + 1, a] for a in range(3))
            up[b][t, 0] = ex + xp(ez, p[b][t + 2, 2]) - ez
            up[b][t, 1] = ey + yp(ez) - ez

        @pl.when(me < n16 - 1)
        def _():
            halo(b, j, True).start()

    def halo_wait(b, j):
        @pl.when(me > 0)
        def _():
            halo(b, j, True).wait_recv()
            halo(b, j, False).wait_send()

        @pl.when(me < n16 - 1)
        def _():
            halo(b, j, False).wait_recv()
            halo(b, j, True).wait_send()

    def curl_tile(b, t):
        at = t + 1
        ex, ey, ez = (p[b][at, a] for a in range(3))
        ex_b, ey_b, ez_b = (p[b][at - 1, a] for a in range(3))
        ey_x = xp(ey, p[b][at + 1, 1])
        ez_x = xp(ez, p[b][at + 1, 2])
        ux, uy = above[b][at, 0], above[b][at, 1]
        v = ey_x - ey
        image_x = 4.0 * ex - yp(ex) - ym(ex + v) + v - ux - below[b][t, 0] + ez_x - ez
        h = ex - xm(ex, ex_b) + ez
        image_y = 4.0 * ey - ey_x - xm(ey, ey_b) - uy - below[b][t, 1] + yp(h) - h
        du = ux - ex
        du_b = above[b][at - 1, 0] - ex_b
        dv = uy - ey
        image_z = (
            4.0 * ez - ez_x - yp(ez) - xm(ez + du, ez_b + du_b) - ym(ez + dv) + du + dv
        )
        return [image_x, image_y, image_z]

    def layer_row(ref, row):
        return jnp.where(core == 0, ref[pl.ds(row, 1), :], ref[pl.ds(row + 1, 1), :])

    def operators(b, j):
        images = [[], [], []]
        for c in range(CHUNK):
            t = CHUNK * j + c
            images[0] += curl_tile(b, t)
            loss = layer_row(sig, 2 * t)
            for a in range(3):
                field = p[b][t + 1, a]
                images[1].append(field * layer_row(eps, 2 * tiles * a + 2 * t))
                images[2].append(field * loss)
        stack = jnp.concatenate([jnp.concatenate(i, axis=1) for i in images], axis=0)
        high, low = split(stack)
        op_hi[b][j] = high
        op_lo[b][j] = low
        t_acc[b][...] += dot_nt(high, bhi[j]) + dot_nt(high, blo[j]) + dot_nt(low, bhi[j])

    def lagged(b, j):
        halo_wait(b, j - 1)
        operators(b, j)

    def all_operators(b):
        halo_wait(b, chunks - 1)
        descending(functools.partial(lagged, b), chunks - 1)
        operators(b, 0)

    def t_copy(b):
        return remote(t_send[b], t_recv[b], t_s.at[b], t_r.at[b], mate)

    def t_start(b):
        for k in range(3):
            total = t_acc[b][q_rows[b] * k : q_rows[b] * (k + 1)]
            t_send[b][k] = jnp.where(core == 0, total[:, own_b:], total[:, :own_b])
        t_copy(b).start()

    per_own = own_b // LANES

    def t_scatter(b):
        t_copy(b).wait()
        blocks = q_rows[b] // SUBS
        for k in range(3):
            total = t_acc[b][q_rows[b] * k : q_rows[b] * (k + 1)]
            mine = jnp.where(core == 0, total[:, :own_b], total[:, own_b:]) + t_recv[b][k]
            for i in range(blocks):
                for c in range(per_own):
                    t_sums[b].put(
                        (k * blocks + i) * per_own + c,
                        mine[SUBS * i : SUBS * (i + 1), LANES * c : LANES * (c + 1)],
                    )
        t_sums[b].scatter()

    def t_rows(b, k):
        blocks = q_rows[b] // SUBS
        rows = []
        for i in range(blocks):
            at = (k * blocks + i) * per_own
            rows.append(
                jnp.concatenate([t_sums[b].get(at + c) for c in range(per_own)], axis=1)
            )
        return jnp.concatenate(rows, axis=0)

    def in_order(parts):
        rows = []
        for e in range(cols):
            for b in batches:
                rows.append(parts[b][widths[b] * e : widths[b] * (e + 1)])
        return jnp.concatenate(rows, axis=0)

    def gram_chunk(j):
        high, low = split(in_order([field_chunk(p[b], j) for b in batches]))
        p2_hi[j] = high
        p2_lo[j] = low
        gram_acc[...] += dot_nt(high, high) + dot_nt(high, low) + dot_nt(low, high)

    def m_chunk(rows_of, j):
        high, low = p2_hi[j], p2_lo[j]
        for b in rows_of:
            m_acc[b][...] += (
                dot_nt(op_hi[b][j], high) + dot_nt(op_hi[b][j], low) + dot_nt(op_lo[b][j], high)
            )

    def s_wait(b):
        for at, copy in s_copies:
            if at == b:
                copy.wait()

    writes = {}

    def write(i):
        writes[i] = pltpu.make_async_copy(stage[i], outs[i], out_s.at[i])
        writes[i].start()

    for b in batches:
        s_wait(b)
        if b == 0:
            meet_wait(3)
            for i in range(4, bits):
                meet_signal(i)
                meet_wait(i)
        first_coef(b)
        if b:
            get_coef(0, b - 1)
            combine(0, b - 1)
        c_sums[0][b].spread()
    second_coef(0)
    get_coef(0, last)
    combine(0, last)
    c_sums[1][0].spread()
    get_coef(1, 0)
    combine(1, 0)
    for b in batches[1:]:
        second_coef(b)
        if b > 1:
            get_coef(1, b - 1)
            combine(1, b - 1)
        c_sums[1][b].spread()
    for b in batches:
        t_acc[b][...] = jnp.zeros_like(t_acc[b])
        m_acc[b][...] = jnp.zeros_like(m_acc[b])
    gram_acc[...] = jnp.zeros_like(gram_acc)
    descending(functools.partial(finish_field, 0))
    get_coef(1, last)
    combine(1, last)

    coef_t[...] = in_order([ct[0][b][...] + ct[1][b][...] for b in batches])
    coef_ref[...] = jnp.where(core == 0, coef_t[:, :own_b], coef_t[:, own_b:]).T
    write(1)

    for b in batches[:-1]:
        then = b + 1
        if then != last:
            finish_field(then, chunks - 1)
            all_operators(b)
            t_start(b)
            for j in reversed(range(chunks - 1)):
                finish_field(then, j)
                if j == chunks - 2:
                    t_scatter(b)
                if j == 1:
                    t_sums[b].spread()
        else:

            halo_wait(b, chunks - 1)

            def both(j):
                lagged(b, j)
                finish_field(then, j)
                gram_chunk(j)
                m_chunk(batches[:-1], j)

            descending(both, chunks - 1)
            operators(b, 0)
            t_start(b)
            finish_field(then, 0)
            gram_chunk(0)
    for i in range(total_s // SUBS):
        g_sum.put(i, gram_acc[SUBS * i : SUBS * (i + 1), :])
    g_sum.scatter()
    t_scatter(last - 1)
    m_chunk(batches[:-1], 0)

    halo_wait(last, chunks - 1)
    descending(functools.partial(lagged, last), chunks - 1)
    g_sum.spread()
    operators(last, 0)
    t_start(last)

    descending(functools.partial(m_chunk, [last]))
    half_s = total_s // 2
    m_halves = []
    for k in range(3):
        rows = in_order([m_acc[b][q_rows[b] * k : q_rows[b] * (k + 1)] for b in batches])
        mine, other = mine_of(rows[:half_s], rows[half_s:])
        m_send[k] = other
        m_halves.append(mine)
    m_copy = remote(m_send, m_recv, m_sems.at[0], m_sems.at[1], mate)
    m_copy.start()
    t_scatter(last)
    m_copy.wait()
    half_blocks = half_s // SUBS
    for k in range(3):
        total = m_halves[k] + m_recv[k]
        for i in range(half_blocks):
            m_sum.put(k * half_blocks + i, total[SUBS * i : SUBS * (i + 1)])
    m_sum.scatter()
    t_sums[last - 1].spread()
    g_sum.finish()

    def between():
        t_sums[last].spread()
        m_sum.spread()

    row_blocks = total_s // SUBS
    gram_rows = [g_sum.get(i) * (1.0 / unknowns) for i in range(row_blocks)]
    for i, value in enumerate(inverse_factor(gram_rows, between)):
        inv_ref[SUBS * i : SUBS * (i + 1)] = value

    def own_rows(which):
        return pl.ds(pl.multiple_of(which * own_s, SUBS), own_s)

    inv_own = inv_ref[own_rows(d), :]
    inv_mate = inv_ref[own_rows(2 * chip + 1 - core), :]
    inv_chip = jnp.concatenate([inv_own, inv_mate], axis=0)

    def nb_copy(j):
        part = pl.ds(CHUNK * j, CHUNK)
        return remote(nb_send.at[part], nb_recv.at[part], n_s.at[j], n_r.at[j], mate)

    def nb_body(j):
        value = exact_dot(dot_nn, inv_chip, (p2_hi[j], p2_lo[j]))
        for i in range(3 * CHUNK):
            t, a = CHUNK * j + i // 3, i % 3
            part = value[:, LANES * i : LANES * (i + 1)]
            nb_own[t, a] = part[:own_s]
            nb_send[t, a] = part[own_s:]
        nb_copy(j).start()

    descending(nb_body)
    inverse = inv_ref[...]
    inverse_halves = split(inverse)

    def nb_out(j):
        nb_copy(j).wait()
        for i in range(3 * CHUNK):
            t, a = CHUNK * j + i // 3, i % 3
            layers = mine_of(nb_own[t, a], nb_recv[t, a])
            for layer in range(2):
                start = (2 * tiles * a + layer) + 2 * t
                nb_ref[pl.ds(start, own_s, stride=per_col), :] = layers[layer]

    descending(nb_out)
    write(0)
    m_sum.finish()
    for k in range(3):
        rows = [m_sum.get(k * half_blocks + i) for i in range(half_blocks)]
        m_send[k] = jnp.concatenate(rows, axis=0)
    m_back = remote(m_send, m_got, m_sems.at[2], m_sems.at[3], mate)
    m_back.start()
    for b in batches:
        t_sums[b].finish()
    for k in range(3):
        cross_ref[k] = exact_dot(dot_nn, inverse, in_order([t_rows(b, k) for b in batches])).T
    write(2)

    m_back.wait()
    for k in range(3):
        rows = jnp.concatenate(mine_of(m_send[k], m_got[k]), axis=0)
        half = exact_dot(dot_nn, inv_own, rows)
        block_ref[k] = exact_dot(dot_nt, half, inverse_halves) * (1.0 / unknowns)
    write(3)
    for copy in writes.values():
        copy.wait()


def hand_over(*refs):
    sources, targets, held, sems = refs[:4], refs[4:8], refs[8:12], refs[12]
    reads = [pltpu.make_async_copy(sources[i], held[i], sems.at[0, i]) for i in range(4)]
    writes = [pltpu.make_async_copy(held[i], targets[i], sems.at[1, i]) for i in range(4)]
    for copy in reads:
        copy.start()
    for read, copy in zip(reads, writes):
        read.wait()
        copy.start()
    for copy in writes:
        copy.wait()


def shards(basis, snapshots, permittivity, labels, sigma_table):
    own_b, own_s = basis.shape[0], snapshots.shape[0]
    layers, layer = basis.shape[2:]
    assert layers == 2
    grid_size, cols = lax.axis_size("grid"), lax.axis_size("cols")
    tiles = layer // LANES
    chips = cols // 2
    n16 = 2 * grid_size
    widths = batch_widths(own_s)
    q_rows = [width * cols for width in widths]
    total_s = own_s * cols
    chip_b = 2 * own_b
    chunks = tiles // CHUNK
    depth = CHUNK * 3 * LANES
    per_col = 6 * tiles
    count = len(widths)

    def rows_of(value):
        lead = value.shape[:-2]
        value = value.reshape(lead + (layers, tiles, LANES))
        return jnp.swapaxes(value, -3, -2).reshape(-1, LANES)

    def vmem(*shape, dtype=F32):
        return pltpu.VMEM(shape, dtype)

    out_shapes = [
        (own_s * per_col, LANES),
        (own_b, total_s),
        (3, own_b, total_s),
        (3, own_s, total_s),
    ]
    scratch = [
        vmem(own_s * per_col, LANES),
        vmem(own_b * per_col, LANES),
        vmem(tiles, 3, own_b, LANES),
        vmem(tiles, 3, own_b, LANES),
        vmem(chunks, chip_b, depth, dtype=BF16),
        vmem(chunks, chip_b, depth, dtype=BF16),
        vmem(chunks, total_s, depth, dtype=BF16),
        vmem(chunks, total_s, depth, dtype=BF16),
        vmem(total_s, chip_b),
        vmem(total_s, total_s),
    ]
    scratch += [vmem(tiles, 3, own_s, LANES)] * 3
    scratch += [vmem(layers * tiles, LANES), vmem(3 * layers * tiles, LANES)]
    scratch += [vmem(layers * tiles, LANES, dtype=labels.dtype)]
    scratch += [pltpu.SMEM(sigma_table.shape, F32), vmem(total_s, total_s)]
    scratch += [vmem(*shape) for shape in out_shapes]
    scratch += [vmem(tiles, 3, width, LANES) for width in widths]
    scratch += [vmem(tiles + 2, 3, q, LANES) for q in q_rows]
    scratch += [vmem(tiles, 2, q, LANES) for q in q_rows] * 2
    scratch += [vmem(tiles + 1, 2, q, LANES) for q in q_rows]
    scratch += [vmem(tiles, 3, q, LANES) for q in q_rows] * 2
    scratch += [vmem(chips - 1, tiles, 3, q, LANES) for q in q_rows] * 2
    scratch += [vmem(q, chip_b) for q in q_rows]
    scratch += [vmem(3 * q, chip_b) for q in q_rows]
    scratch += [vmem(3, q, own_b) for q in q_rows] * 2
    scratch += [vmem(chunks, 3 * q, depth, dtype=BF16) for q in q_rows] * 2
    scratch += [vmem(3 * q, total_s) for q in q_rows]
    scratch += [vmem(q, chip_b) for q in q_rows] * 2
    sem = pltpu.SemaphoreType.DMA
    scratch += [sem((5,)), sem((4,))]
    scratch += [sem((count, 2 * chips - 1))] * 2
    scratch += [sem((tiles,))] * 2
    scratch += [sem((2, count, chips - 1, chunks))] * 2
    scratch += [sem((count, 2, chunks))] * 2
    scratch += [sem((count,))] * 2
    scratch += [sem((chunks,))] * 2
    scratch += [pltpu.SemaphoreType.REGULAR((log2(n16),))]
    vreg = SUBS * LANES
    for _ in range(2):
        for q in q_rows:
            scratch += reduction_scratch(n16, q * chip_b // vreg)
    for q in q_rows:
        scratch += reduction_scratch(grid_size, 3 * q * own_b // vreg)
    scratch += reduction_scratch(n16, total_s * total_s // vreg)
    scratch += reduction_scratch(grid_size, 3 * total_s * total_s // 2 // vreg)
    scratch += [vmem(3, total_s // 2, total_s)] * 3 + [sem((4,))]

    anywhere = pl.BlockSpec(memory_space=pl.ANY)
    outputs = [jax.ShapeDtypeStruct(shape, F32) for shape in out_shapes]
    dims = (grid_size, cols, own_b, own_s, tiles)
    results = pl.pallas_call(
        functools.partial(kernel, dims),
        out_shape=outputs,
        in_specs=[anywhere] * 5,
        out_specs=[anywhere] * 4,
        scratch_shapes=scratch,
        compiler_params=pltpu.CompilerParams(
            collective_id=0, has_side_effects=True, vmem_limit_bytes=62 << 20
        ),
    )(
        rows_of(basis),
        rows_of(snapshots),
        rows_of(permittivity),
        rows_of(labels),
        sigma_table,
    )
    new_rows, coefficients, cross_terms, block_terms = pl.pallas_call(
        hand_over,
        out_shape=outputs,
        in_specs=[anywhere] * 4,
        out_specs=[anywhere] * 4,
        scratch_shapes=[vmem(*shape) for shape in out_shapes] + [sem((2, 4))],
    )(*results)
    new_basis = jnp.swapaxes(
        new_rows.reshape(own_s, 3, tiles, layers, LANES), 2, 3
    ).reshape(snapshots.shape)
    return (new_basis, coefficients, cross_terms, block_terms)


def solution(mesh):
    placed = (
        P("cols", None, "grid", None),
        P("cols", None, "grid", None),
        P(None, "grid", None),
        P("grid", None),
        P(),
    )
    return jax.shard_map(
        shards,
        mesh=mesh,
        in_specs=placed,
        out_specs=(
            P("cols", None, "grid", None),
            P("cols", None),
            P(None, "cols", None),
            P(None, "cols", None),
        ),
        check_vma=False,
    )
```

```python
import functools

import jax
import jax.numpy as jnp
from jax import lax
from jax.experimental import pallas as pl
from jax.experimental.pallas import tpu as pltpu
from jax.sharding import PartitionSpec as P

NY = 32
LANES = 128
SUBS = 8
CHUNK = 2
PIVOTS = 4
MESH = pl.DeviceIdType.MESH
F32 = jnp.float32
BF16 = jnp.bfloat16


def split(value):
    high = value.astype(BF16)
    return high, (value - high.astype(F32)).astype(BF16)


def dot_nt(left, right):
    return lax.dot_general(
        left, right, (((1,), (1,)), ((), ())), preferred_element_type=F32
    )


def dot_nn(left, right):
    return lax.dot_general(
        left, right, (((1,), (0,)), ((), ())), preferred_element_type=F32
    )


def exact_dot(dot, left, right):
    rows = left.shape[0]
    stacked = jnp.concatenate(split(left), axis=0)
    high, low = right if isinstance(right, tuple) else split(right)
    total = dot(stacked, high) + dot(stacked, low)
    return total[:rows] + total[rows:]


def inverse_factor(rows, between):
    count = len(rows)
    size = count * SUBS
    shape = (SUBS, size)
    left = list(rows)
    lane = lax.broadcasted_iota(jnp.int32, shape, 1)
    sub = lax.broadcasted_iota(jnp.int32, shape, 0)
    right = [jnp.where(lane == sub + SUBS * i, 1.0, 0.0).astype(F32) for i in range(count)]

    def spread(value):
        return jnp.broadcast_to(value, shape)

    for k in range(0, size, PIVOTS):
        if k == size * 3 // 4:
            between()
        block, first = divmod(k, SUBS)
        row_l = [spread(left[block][first + t : first + t + 1]) for t in range(PIVOTS)]
        row_r = [spread(right[block][first + t : first + t + 1]) for t in range(PIVOTS)]
        pivot = {
            (s, t): spread(row_l[s][:, k + t : k + t + 1])
            for s in range(PIVOTS)
            for t in range(s + 1)
        }
        scale, factor = [], {}
        for t in range(PIVOTS):
            scale.append(lax.rsqrt(pivot[t, t]))
            row_l[t] = row_l[t] * scale[t]
            row_r[t] = row_r[t] * scale[t]
            for s in range(t + 1, PIVOTS):
                factor[s, t] = pivot[s, t] * scale[t]
            for s in range(t + 1, PIVOTS):
                for u in range(t + 1, s + 1):
                    pivot[s, u] = pivot[s, u] - factor[s, t] * factor[u, t]
                row_l[s] = row_l[s] - factor[s, t] * row_l[t]
                row_r[s] = row_r[s] - factor[s, t] * row_r[t]
        for at in range(block, count):
            inside = at == block
            if not inside or first + PIVOTS < SUBS:
                cols = [spread(left[at][:, k + t : k + t + 1]) for t in range(PIVOTS)]
                for t in range(PIVOTS):
                    cols[t] = cols[t] * scale[t]
                    for s in range(t + 1, PIVOTS):
                        cols[s] = cols[s] - factor[s, t] * cols[t]
                if inside:
                    cols = [jnp.where(sub >= first + PIVOTS, c, 0.0) for c in cols]
                for t in range(PIVOTS):
                    left[at] = left[at] - cols[t] * row_l[t]
                    right[at] = right[at] - cols[t] * row_r[t]
            if inside:
                for t in range(PIVOTS):
                    right[at] = jnp.where(sub == first + t, row_r[t], right[at])
    return right


def remote(src, dst, send_sem, recv_sem, peer):
    return pltpu.make_async_remote_copy(
        src_ref=src,
        dst_ref=dst,
        send_sem=send_sem,
        recv_sem=recv_sem,
        device_id=peer,
        device_id_type=MESH,
    )


class Reduction:
    def __init__(self, refs, n, me, peer):
        self.x, self.slots, self.o, self.sems = refs
        self.n, self.me, self.peer = n, me, peer

    def put(self, at, value):
        blocks = self.x.shape[1]
        self.x[at // blocks, at % blocks] = value

    def get(self, at):
        blocks = self.x.shape[1]
        return self.o[at // blocks, at % blocks]

    def scatter(self):
        def body(k, carry):
            q = lax.rem(self.me + k, self.n)
            remote(
                self.x.at[q], self.slots.at[k - 1], self.sems.at[0], self.sems.at[1], self.peer(q)
            ).start()
            return carry

        lax.fori_loop(1, self.n, body, 0)

    def spread(self):
        whole = remote(self.slots, self.slots, self.sems.at[0], self.sems.at[1], self.peer(self.me))
        whole.wait_recv()
        self.o[self.me] = self.x[self.me] + jnp.sum(self.slots[...], axis=0)

        def body(k, carry):
            q = lax.rem(self.me + k, self.n)
            mine = self.o.at[self.me]
            remote(mine, mine, self.sems.at[2], self.sems.at[3], self.peer(q)).start()
            return carry

        lax.fori_loop(1, self.n, body, 0)

    def finish(self):
        sent = remote(self.slots, self.slots, self.sems.at[0], self.sems.at[1], self.peer(self.me))
        sent.wait_send()
        rest = self.o.at[pl.ds(0, self.n - 1)]
        whole = remote(rest, rest, self.sems.at[2], self.sems.at[3], self.peer(self.me))
        whole.wait_recv()
        whole.wait_send()


def reduction_scratch(n, blocks):
    piece = -(-blocks // n)
    shapes = [(n, piece), (n - 1, piece), (n, piece)]
    return [pltpu.VMEM(s + (SUBS, LANES), F32) for s in shapes] + [pltpu.SemaphoreType.DMA((4,))]


def batch_widths(own_s):
    if own_s % (4 * SUBS) == 0:
        return (own_s // 4, own_s // 2, own_s // 4)
    return (own_s // 2, own_s // 2)


def log2(n):
    bits = n.bit_length() - 1
    assert n == 1 << bits
    return bits


def kernel(dims, b_ref, s_ref, eps_ref, lab_ref, sig_ref, *rest):
    (grid_size, cols, own_b, own_s, tiles) = dims
    chips = cols // 2
    n16 = 2 * grid_size
    bits = log2(n16)
    widths = batch_widths(own_s)
    starts = [sum(widths[:b]) for b in range(len(widths))]
    batches = range(len(widths))
    last = len(widths) - 1
    q_rows = [width * cols for width in widths]
    total_s = own_s * cols
    chip_b = 2 * own_b
    chunks = tiles // CHUNK
    per_col = 6 * tiles
    unknowns = 3 * tiles * LANES * n16

    outs = rest[:4]
    refs = list(rest[4:])

    def take(count):
        out = refs[:count]
        del refs[:count]
        return out

    def each():
        return take(len(widths))

    sland, bland, bsend, brecv, bhi, blo, p2_hi, p2_lo, coef_t, inv_ref = take(10)
    nb_own, nb_send, nb_recv, sig, eps, lab, table, gram_acc = take(8)
    stage = take(4)
    nb_ref, coef_ref, cross_ref, block_ref = stage
    ssend, p, up, below, above = each(), each(), each(), each(), each()
    uown, urecv = [each(), each()], [each(), each()]
    acc, t_acc, t_send, t_recv, op_hi, op_lo, m_acc = (each() for _ in range(7))
    ct = [each(), each()]
    (loc, out_s, s_s, s_r, bm_s, bm_r, u_s, u_r, h_s, h_r, t_s, t_r, n_s, n_r, meet) = take(15)

    g = lax.axis_index("grid")
    d = lax.axis_index("cols")
    chip, core = d // 2, lax.rem(d, 2)
    me = 2 * g + core
    mate = (g, 2 * chip + 1 - core)
    far = [lax.rem(chip + k, chips) for k in range(1, chips)]
    same = [(g, 2 * y + core) for y in far]
    cross = [(g, 2 * y + 1 - core) for y in far]

    def line(q):
        return (q // 2, 2 * chip + lax.rem(q, 2))

    def slab(q):
        return (q, d)

    c_sums = [[Reduction(take(4), n16, me, line) for _ in batches] for _ in range(2)]
    t_sums = [Reduction(take(4), grid_size, g, slab) for _ in batches]
    g_sum = Reduction(take(4), n16, me, line)
    m_sum = Reduction(take(4), grid_size, g, slab)
    m_send, m_recv, m_got, m_sems = take(4)

    partners = [
        line(me + (1 << i) * (1 - 2 * lax.rem(me // (1 << i), 2))) for i in range(bits)
    ]
    barrier = pltpu.get_barrier_semaphore()
    for peer in same + cross + partners:
        pl.semaphore_signal(barrier, inc=1, device_id=peer, device_id_type=MESH)

    def meet_signal(i):
        if i < bits:
            pl.semaphore_signal(meet.at[i], inc=1, device_id=partners[i], device_id_type=MESH)

    def meet_wait(i):
        if i < bits:
            pl.semaphore_wait(meet.at[i], 1)

    loads = [
        pltpu.make_async_copy(src, dst, loc.at[i])
        for i, (src, dst) in enumerate(
            [(s_ref, sland), (b_ref, bland), (eps_ref, eps), (lab_ref, lab), (sig_ref, table)]
        )
    ]
    for load in loads:
        load.start()

    for b in batches:
        zero = jnp.zeros((3, q_rows[b], LANES), F32)
        for edge in (0, tiles + 1):
            p[b][edge] = zero
        above[b][0] = zero[:2]

        @pl.when(me == 0)
        def _():
            below[b][...] = jnp.zeros(below[b].shape, F32)

        @pl.when(me == n16 - 1)
        def _():
            above[b][...] = jnp.zeros(above[b].shape, F32)

    def mine_of(first, second):
        return jnp.where(core == 0, first, second), jnp.where(core == 0, second, first)

    loads[0].wait()

    def my_cols(b):
        return pl.ds(pl.multiple_of(d * widths[b], SUBS), widths[b])

    for b in batches:

        def sort_s(t, carry):
            for a in range(3):
                layers = []
                for layer in range(2):
                    start = starts[b] * per_col + (2 * tiles * a + layer) + 2 * t
                    layers.append(sland[pl.ds(start, widths[b], stride=per_col), :])
                own, other = mine_of(*layers)
                p[b][t + 1, a, my_cols(b), :] = own
                ssend[b][t, a] = other
            return carry

        lax.fori_loop(0, tiles, sort_s, 0)

    pl.semaphore_wait(barrier, 2 * (chips - 1) + bits)
    s_copies = []
    for b in batches:
        landing = p[b].at[pl.ds(1, tiles), :, my_cols(b), :]
        plan = [(landing, peer) for peer in same]
        plan += [(ssend[b], peer) for peer in cross + [mate]]
        for i, (src, peer) in enumerate(plan):
            copy = remote(src, landing, s_s.at[b, i], s_r.at[b, i], peer)
            copy.start()
            s_copies.append((b, copy))
    meet_signal(0)

    def b_rows(which):
        return pl.ds(pl.multiple_of(which * own_b, own_b), own_b)

    def put_b(t, a, which, value):
        high, low = split(value)
        lanes = pl.ds(pl.multiple_of((lax.rem(t, CHUNK) * 3 + a) * LANES, LANES), LANES)
        bhi[t // CHUNK, b_rows(which), lanes] = high
        blo[t // CHUNK, b_rows(which), lanes] = low

    def sort_b(t, carry):
        for a in range(3):
            layers = []
            for layer in range(2):
                start = (2 * tiles * a + layer) + 2 * t
                layers.append(bland[pl.ds(start, own_b, stride=per_col), :])
            own, other = mine_of(*layers)
            bsend[t, a] = other
            put_b(t, a, core, own)
        remote(bsend.at[t], brecv.at[t], bm_s.at[t], bm_r.at[t], mate).start()
        return carry

    loads[1].wait()
    lax.fori_loop(0, tiles, sort_b, 0)
    meet_wait(0)
    meet_signal(1)

    def mate_b(t, carry):
        remote(bsend.at[t], brecv.at[t], bm_s.at[t], bm_r.at[t], mate).wait()
        for a in range(3):
            put_b(t, a, 1 - core, brecv[t, a])
        return carry

    lax.fori_loop(0, tiles // 2, mate_b, 0)
    meet_wait(1)
    meet_signal(2)
    lax.fori_loop(tiles // 2, tiles, mate_b, 0)
    meet_wait(2)
    meet_signal(3)

    for load in loads[2:]:
        load.wait()
    region = lab[...]
    picked = jnp.zeros(region.shape, F32)
    for k in range(sig_ref.shape[0]):
        picked = jnp.where(region == k, table[k], picked)
    sig[...] = picked

    def field_chunk(buffer, j):
        parts = [buffer[CHUNK * j + i // 3 + 1, i % 3] for i in range(3 * CHUNK)]
        return jnp.concatenate(parts, axis=1)

    per_row = chip_b // LANES

    def put_coef(total, sweep, b):
        work = c_sums[sweep][b]
        for i in range(q_rows[b] // SUBS):
            for k in range(per_row):
                work.put(
                    i * per_row + k,
                    total[SUBS * i : SUBS * (i + 1), LANES * k : LANES * (k + 1)],
                )
        work.scatter()

    def get_coef(sweep, b):
        work = c_sums[sweep][b]
        work.finish()
        rows = []
        for i in range(q_rows[b] // SUBS):
            rows.append(
                jnp.concatenate([work.get(i * per_row + k) for k in range(per_row)], axis=1)
            )
        ct[sweep][b][...] = jnp.concatenate(rows, axis=0)

    def descending(body, count=chunks):
        def step(i, carry):
            body(chunks - 1 - i)
            return carry

        lax.fori_loop(0, count, step, 0)

    def first_coef(b):
        acc[b][...] = jnp.zeros_like(acc[b])

        def body(j):
            acc[b][...] += exact_dot(dot_nt, field_chunk(p[b], j), (bhi[j], blo[j]))

        descending(body)
        put_coef(acc[b][...], 0, b)

    def u_copy(sweep, b, j, k):
        part = pl.ds(CHUNK * j, CHUNK)
        return remote(
            uown[sweep][b].at[part],
            urecv[sweep][b].at[k, part],
            u_s.at[sweep, b, k, j],
            u_r.at[sweep, b, k, j],
            same[k],
        )

    def combine(sweep, b):
        weights = ct[sweep][b][...]

        def body(j):
            u = exact_dot(dot_nn, weights, (bhi[j], blo[j]))
            for i in range(3 * CHUNK):
                uown[sweep][b][CHUNK * j + i // 3, i % 3] = u[:, LANES * i : LANES * (i + 1)]
            for k in range(chips - 1):
                u_copy(sweep, b, j, k).start()

        descending(body)

    def remove(sweep, b, j):
        for k in range(chips - 1):
            u_copy(sweep, b, j, k).wait()
        parts = []
        for i in range(3 * CHUNK):
            t, a = CHUNK * j + i // 3, i % 3
            total = uown[sweep][b][t, a]
            for k in range(chips - 1):
                total = total + urecv[sweep][b][k, t, a]
            left = p[b][t + 1, a] - total
            p[b][t + 1, a] = left
            parts.append(left)
        return parts

    def second_coef(b):
        acc[b][...] = jnp.zeros_like(acc[b])

        def body(j):
            field = jnp.concatenate(remove(0, b, j), axis=1)
            acc[b][...] += exact_dot(dot_nt, field, (bhi[j], blo[j]))

        descending(body)
        put_coef(acc[b][...], 1, b)

    lane = lax.broadcasted_iota(jnp.int32, (max(q_rows), LANES), 1)
    y_at = lax.rem(lane, NY)
    y_top, y_low = y_at != NY - 1, y_at != 0
    x_low, x_top = lane < NY, lane >= LANES - NY

    def yp(f):
        return jnp.where(y_top[: f.shape[0]], pltpu.roll(f, LANES - 1, 1), 0.0)

    def ym(f):
        return jnp.where(y_low[: f.shape[0]], pltpu.roll(f, 1, 1), 0.0)

    def xp(f, after):
        return pltpu.roll(jnp.where(x_low[: f.shape[0]], after, f), LANES - NY, 1)

    def xm(f, before):
        return pltpu.roll(jnp.where(x_top[: f.shape[0]], before, f), NY, 1)

    def halo(b, j, to_next):
        part = pl.ds(CHUNK * j, CHUNK)
        shifted = pl.ds(CHUNK * j + 1, CHUNK)
        if to_next:
            src, dst = up[b].at[part], below[b].at[part]
        else:
            src, dst = p[b].at[shifted, pl.ds(0, 2)], above[b].at[shifted]
        at = 0 if to_next else 1
        return remote(
            src, dst, h_s.at[b, at, j], h_r.at[b, at, j], line(me + 1 if to_next else me - 1)
        )

    def finish_field(b, j):
        remove(1, b, j)

        @pl.when(me > 0)
        def _():
            halo(b, j, False).start()

        for c in range(CHUNK):
            t = CHUNK * j + c
            ex, ey, ez = (p[b][t + 1, a] for a in range(3))
            up[b][t, 0] = ex + xp(ez, p[b][t + 2, 2]) - ez
            up[b][t, 1] = ey + yp(ez) - ez

        @pl.when(me < n16 - 1)
        def _():
            halo(b, j, True).start()

    def halo_wait(b, j):
        @pl.when(me > 0)
        def _():
            halo(b, j, True).wait_recv()
            halo(b, j, False).wait_send()

        @pl.when(me < n16 - 1)
        def _():
            halo(b, j, False).wait_recv()
            halo(b, j, True).wait_send()

    def curl_tile(b, t):
        at = t + 1
        ex, ey, ez = (p[b][at, a] for a in range(3))
        ex_b, ey_b, ez_b = (p[b][at - 1, a] for a in range(3))
        ey_x = xp(ey, p[b][at + 1, 1])
        ez_x = xp(ez, p[b][at + 1, 2])
        ux, uy = above[b][at, 0], above[b][at, 1]
        v = ey_x - ey
        image_x = 4.0 * ex - yp(ex) - ym(ex + v) + v - ux - below[b][t, 0] + ez_x - ez
        h = ex - xm(ex, ex_b) + ez
        image_y = 4.0 * ey - ey_x - xm(ey, ey_b) - uy - below[b][t, 1] + yp(h) - h
        du = ux - ex
        du_b = above[b][at - 1, 0] - ex_b
        dv = uy - ey
        image_z = (
            4.0 * ez - ez_x - yp(ez) - xm(ez + du, ez_b + du_b) - ym(ez + dv) + du + dv
        )
        return [image_x, image_y, image_z]

    def layer_row(ref, row):
        return jnp.where(core == 0, ref[pl.ds(row, 1), :], ref[pl.ds(row + 1, 1), :])

    def operators(b, j):
        images = [[], [], []]
        for c in range(CHUNK):
            t = CHUNK * j + c
            images[0] += curl_tile(b, t)
            loss = layer_row(sig, 2 * t)
            for a in range(3):
                field = p[b][t + 1, a]
                images[1].append(field * layer_row(eps, 2 * tiles * a + 2 * t))
                images[2].append(field * loss)
        stack = jnp.concatenate([jnp.concatenate(i, axis=1) for i in images], axis=0)
        high, low = split(stack)
        op_hi[b][j] = high
        op_lo[b][j] = low
        t_acc[b][...] += dot_nt(high, bhi[j]) + dot_nt(high, blo[j]) + dot_nt(low, bhi[j])

    def lagged(b, j):
        halo_wait(b, j - 1)
        operators(b, j)

    def all_operators(b):
        halo_wait(b, chunks - 1)
        descending(functools.partial(lagged, b), chunks - 1)
        operators(b, 0)

    def t_copy(b):
        return remote(t_send[b], t_recv[b], t_s.at[b], t_r.at[b], mate)

    def t_start(b):
        for k in range(3):
            total = t_acc[b][q_rows[b] * k : q_rows[b] * (k + 1)]
            t_send[b][k] = jnp.where(core == 0, total[:, own_b:], total[:, :own_b])
        t_copy(b).start()

    per_own = own_b // LANES

    def t_scatter(b):
        t_copy(b).wait()
        blocks = q_rows[b] // SUBS
        for k in range(3):
            total = t_acc[b][q_rows[b] * k : q_rows[b] * (k + 1)]
            mine = jnp.where(core == 0, total[:, :own_b], total[:, own_b:]) + t_recv[b][k]
            for i in range(blocks):
                for c in range(per_own):
                    t_sums[b].put(
                        (k * blocks + i) * per_own + c,
                        mine[SUBS * i : SUBS * (i + 1), LANES * c : LANES * (c + 1)],
                    )
        t_sums[b].scatter()

    def t_rows(b, k):
        blocks = q_rows[b] // SUBS
        rows = []
        for i in range(blocks):
            at = (k * blocks + i) * per_own
            rows.append(
                jnp.concatenate([t_sums[b].get(at + c) for c in range(per_own)], axis=1)
            )
        return jnp.concatenate(rows, axis=0)

    def in_order(parts):
        rows = []
        for e in range(cols):
            for b in batches:
                rows.append(parts[b][widths[b] * e : widths[b] * (e + 1)])
        return jnp.concatenate(rows, axis=0)

    def gram_chunk(j):
        high, low = split(in_order([field_chunk(p[b], j) for b in batches]))
        p2_hi[j] = high
        p2_lo[j] = low
        gram_acc[...] += dot_nt(high, high) + dot_nt(high, low) + dot_nt(low, high)

    def m_chunk(rows_of, j):
        high, low = p2_hi[j], p2_lo[j]
        for b in rows_of:
            m_acc[b][...] += (
                dot_nt(op_hi[b][j], high) + dot_nt(op_hi[b][j], low) + dot_nt(op_lo[b][j], high)
            )

    def s_wait(b):
        for at, copy in s_copies:
            if at == b:
                copy.wait()

    writes = {}

    def write(i):
        writes[i] = pltpu.make_async_copy(stage[i], outs[i], out_s.at[i])
        writes[i].start()

    for b in batches:
        s_wait(b)
        if b == 0:
            meet_wait(3)
            for i in range(4, bits):
                meet_signal(i)
                meet_wait(i)
        first_coef(b)
        if b:
            get_coef(0, b - 1)
            combine(0, b - 1)
        c_sums[0][b].spread()
    second_coef(0)
    get_coef(0, last)
    combine(0, last)
    c_sums[1][0].spread()
    get_coef(1, 0)
    combine(1, 0)
    for b in batches[1:]:
        second_coef(b)
        if b > 1:
            get_coef(1, b - 1)
            combine(1, b - 1)
        c_sums[1][b].spread()
    for b in batches:
        t_acc[b][...] = jnp.zeros_like(t_acc[b])
        m_acc[b][...] = jnp.zeros_like(m_acc[b])
    gram_acc[...] = jnp.zeros_like(gram_acc)
    descending(functools.partial(finish_field, 0))
    get_coef(1, last)
    combine(1, last)

    coef_t[...] = in_order([ct[0][b][...] + ct[1][b][...] for b in batches])
    coef_ref[...] = jnp.where(core == 0, coef_t[:, :own_b], coef_t[:, own_b:]).T
    write(1)

    for b in batches[:-1]:
        then = b + 1
        if then != last:
            finish_field(then, chunks - 1)
            all_operators(b)
            t_start(b)
            for j in reversed(range(chunks - 1)):
                finish_field(then, j)
                if j == chunks - 2:
                    t_scatter(b)
                if j == 1:
                    t_sums[b].spread()
        else:

            halo_wait(b, chunks - 1)

            def both(j):
                lagged(b, j)
                finish_field(then, j)
                gram_chunk(j)
                m_chunk(batches[:-1], j)

            descending(both, chunks - 1)
            operators(b, 0)
            t_start(b)
            finish_field(then, 0)
            gram_chunk(0)
    for i in range(total_s // SUBS):
        g_sum.put(i, gram_acc[SUBS * i : SUBS * (i + 1), :])
    g_sum.scatter()
    t_scatter(last - 1)
    m_chunk(batches[:-1], 0)

    halo_wait(last, chunks - 1)
    descending(functools.partial(lagged, last), chunks - 1)
    g_sum.spread()
    operators(last, 0)
    t_start(last)

    descending(functools.partial(m_chunk, [last]))
    half_s = total_s // 2
    m_halves = []
    for k in range(3):
        rows = in_order([m_acc[b][q_rows[b] * k : q_rows[b] * (k + 1)] for b in batches])
        mine, other = mine_of(rows[:half_s], rows[half_s:])
        m_send[k] = other
        m_halves.append(mine)
    m_copy = remote(m_send, m_recv, m_sems.at[0], m_sems.at[1], mate)
    m_copy.start()
    t_scatter(last)
    m_copy.wait()
    half_blocks = half_s // SUBS
    for k in range(3):
        total = m_halves[k] + m_recv[k]
        for i in range(half_blocks):
            m_sum.put(k * half_blocks + i, total[SUBS * i : SUBS * (i + 1)])
    m_sum.scatter()
    t_sums[last - 1].spread()
    g_sum.finish()

    def between():
        t_sums[last].spread()
        m_sum.spread()

    row_blocks = total_s // SUBS
    gram_rows = [g_sum.get(i) * (1.0 / unknowns) for i in range(row_blocks)]
    for i, value in enumerate(inverse_factor(gram_rows, between)):
        inv_ref[SUBS * i : SUBS * (i + 1)] = value

    def own_rows(which):
        return pl.ds(pl.multiple_of(which * own_s, SUBS), own_s)

    inv_own = inv_ref[own_rows(d), :]
    inv_mate = inv_ref[own_rows(2 * chip + 1 - core), :]
    inv_chip = jnp.concatenate([inv_own, inv_mate], axis=0)

    def nb_copy(j):
        part = pl.ds(CHUNK * j, CHUNK)
        return remote(nb_send.at[part], nb_recv.at[part], n_s.at[j], n_r.at[j], mate)

    def nb_body(j):
        value = exact_dot(dot_nn, inv_chip, (p2_hi[j], p2_lo[j]))
        for i in range(3 * CHUNK):
            t, a = CHUNK * j + i // 3, i % 3
            part = value[:, LANES * i : LANES * (i + 1)]
            nb_own[t, a] = part[:own_s]
            nb_send[t, a] = part[own_s:]
        nb_copy(j).start()

    descending(nb_body)
    inverse = inv_ref[...]
    inverse_halves = split(inverse)

    def nb_out(j):
        nb_copy(j).wait()
        for i in range(3 * CHUNK):
            t, a = CHUNK * j + i // 3, i % 3
            layers = mine_of(nb_own[t, a], nb_recv[t, a])
            for layer in range(2):
                start = (2 * tiles * a + layer) + 2 * t
                nb_ref[pl.ds(start, own_s, stride=per_col), :] = layers[layer]

    descending(nb_out)
    write(0)
    m_sum.finish()
    for k in range(3):
        rows = [m_sum.get(k * half_blocks + i) for i in range(half_blocks)]
        m_send[k] = jnp.concatenate(rows, axis=0)
    m_back = remote(m_send, m_got, m_sems.at[2], m_sems.at[3], mate)
    m_back.start()
    for b in batches:
        t_sums[b].finish()
    for k in range(3):
        cross_ref[k] = exact_dot(dot_nn, inverse, in_order([t_rows(b, k) for b in batches])).T
    write(2)

    m_back.wait()
    for k in range(3):
        rows = jnp.concatenate(mine_of(m_send[k], m_got[k]), axis=0)
        half = exact_dot(dot_nn, inv_own, rows)
        block_ref[k] = exact_dot(dot_nt, half, inverse_halves) * (1.0 / unknowns)
    write(3)
    for copy in writes.values():
        copy.wait()


def hand_over(*refs):
    sources, targets, held, sems = refs[:4], refs[4:8], refs[8:12], refs[12]
    reads = [pltpu.make_async_copy(sources[i], held[i], sems.at[0, i]) for i in range(4)]
    writes = [pltpu.make_async_copy(held[i], targets[i], sems.at[1, i]) for i in range(4)]
    for copy in reads:
        copy.start()
    for read, copy in zip(reads, writes):
        read.wait()
        copy.start()
    for copy in writes:
        copy.wait()


def shards(basis, snapshots, permittivity, labels, sigma_table):
    own_b, own_s = basis.shape[0], snapshots.shape[0]
    layers, layer = basis.shape[2:]
    assert layers == 2
    grid_size, cols = lax.axis_size("grid"), lax.axis_size("cols")
    tiles = layer // LANES
    chips = cols // 2
    n16 = 2 * grid_size
    widths = batch_widths(own_s)
    q_rows = [width * cols for width in widths]
    total_s = own_s * cols
    chip_b = 2 * own_b
    chunks = tiles // CHUNK
    depth = CHUNK * 3 * LANES
    per_col = 6 * tiles
    count = len(widths)

    def rows_of(value):
        lead = value.shape[:-2]
        value = value.reshape(lead + (layers, tiles, LANES))
        return jnp.swapaxes(value, -3, -2).reshape(-1, LANES)

    def vmem(*shape, dtype=F32):
        return pltpu.VMEM(shape, dtype)

    out_shapes = [
        (own_s * per_col, LANES),
        (own_b, total_s),
        (3, own_b, total_s),
        (3, own_s, total_s),
    ]
    scratch = [
        vmem(own_s * per_col, LANES),
        vmem(own_b * per_col, LANES),
        vmem(tiles, 3, own_b, LANES),
        vmem(tiles, 3, own_b, LANES),
        vmem(chunks, chip_b, depth, dtype=BF16),
        vmem(chunks, chip_b, depth, dtype=BF16),
        vmem(chunks, total_s, depth, dtype=BF16),
        vmem(chunks, total_s, depth, dtype=BF16),
        vmem(total_s, chip_b),
        vmem(total_s, total_s),
    ]
    scratch += [vmem(tiles, 3, own_s, LANES)] * 3
    scratch += [vmem(layers * tiles, LANES), vmem(3 * layers * tiles, LANES)]
    scratch += [vmem(layers * tiles, LANES, dtype=labels.dtype)]
    scratch += [pltpu.SMEM(sigma_table.shape, F32), vmem(total_s, total_s)]
    scratch += [vmem(*shape) for shape in out_shapes]
    scratch += [vmem(tiles, 3, width, LANES) for width in widths]
    scratch += [vmem(tiles + 2, 3, q, LANES) for q in q_rows]
    scratch += [vmem(tiles, 2, q, LANES) for q in q_rows] * 2
    scratch += [vmem(tiles + 1, 2, q, LANES) for q in q_rows]
    scratch += [vmem(tiles, 3, q, LANES) for q in q_rows] * 2
    scratch += [vmem(chips - 1, tiles, 3, q, LANES) for q in q_rows] * 2
    scratch += [vmem(q, chip_b) for q in q_rows]
    scratch += [vmem(3 * q, chip_b) for q in q_rows]
    scratch += [vmem(3, q, own_b) for q in q_rows] * 2
    scratch += [vmem(chunks, 3 * q, depth, dtype=BF16) for q in q_rows] * 2
    scratch += [vmem(3 * q, total_s) for q in q_rows]
    scratch += [vmem(q, chip_b) for q in q_rows] * 2
    sem = pltpu.SemaphoreType.DMA
    scratch += [sem((5,)), sem((4,))]
    scratch += [sem((count, 2 * chips - 1))] * 2
    scratch += [sem((tiles,))] * 2
    scratch += [sem((2, count, chips - 1, chunks))] * 2
    scratch += [sem((count, 2, chunks))] * 2
    scratch += [sem((count,))] * 2
    scratch += [sem((chunks,))] * 2
    scratch += [pltpu.SemaphoreType.REGULAR((log2(n16),))]
    vreg = SUBS * LANES
    for _ in range(2):
        for q in q_rows:
            scratch += reduction_scratch(n16, q * chip_b // vreg)
    for q in q_rows:
        scratch += reduction_scratch(grid_size, 3 * q * own_b // vreg)
    scratch += reduction_scratch(n16, total_s * total_s // vreg)
    scratch += reduction_scratch(grid_size, 3 * total_s * total_s // 2 // vreg)
    scratch += [vmem(3, total_s // 2, total_s)] * 3 + [sem((4,))]

    anywhere = pl.BlockSpec(memory_space=pl.ANY)
    outputs = [jax.ShapeDtypeStruct(shape, F32) for shape in out_shapes]
    dims = (grid_size, cols, own_b, own_s, tiles)
    results = pl.pallas_call(
        functools.partial(kernel, dims),
        out_shape=outputs,
        in_specs=[anywhere] * 5,
        out_specs=[anywhere] * 4,
        scratch_shapes=scratch,
        compiler_params=pltpu.CompilerParams(
            collective_id=0, has_side_effects=True, vmem_limit_bytes=62 << 20
        ),
    )(
        rows_of(basis),
        rows_of(snapshots),
        rows_of(permittivity),
        rows_of(labels),
        sigma_table,
    )
    new_rows, coefficients, cross_terms, block_terms = pl.pallas_call(
        hand_over,
        out_shape=outputs,
        in_specs=[anywhere] * 4,
        out_specs=[anywhere] * 4,
        scratch_shapes=[vmem(*shape) for shape in out_shapes] + [sem((2, 4))],
    )(*results)
    new_basis = jnp.swapaxes(
        new_rows.reshape(own_s, 3, tiles, layers, LANES), 2, 3
    ).reshape(snapshots.shape)
    return (new_basis, coefficients, cross_terms, block_terms)


def solution(mesh):
    placed = (
        P("cols", None, "grid", None),
        P("cols", None, "grid", None),
        P(None, "grid", None),
        P("grid", None),
        P(),
    )
    return jax.shard_map(
        shards,
        mesh=mesh,
        in_specs=placed,
        out_specs=(
            P("cols", None, "grid", None),
            P("cols", None),
            P(None, "cols", None),
            P(None, "cols", None),
        ),
        check_vma=False,
    )
```
